512 devices in a mesh: inline: 8 (over y, x_hi), window: 16 (over z), replica: 4 (over x_lo, core).
Axes of the slice: x: 4 (x_hi: 2, x_lo: 2; x = x_hi * 2 + x_lo), y: 4, z: 16, core: 2. Of those that a mesh axis runs over, the one named last changes fastest.
Arguments:
- tokens: bfloat16 [512, 128, 8, 512], P(('replica', 'inline', 'window')), parts along dimension 0, may hold values from -6 to 6
- probe_match_payload_matrix: bfloat16 [512, 1536], replicated, may hold values from -1.5 to 1.5
- w_out: bfloat16 [512, 512], replicated, may hold values from -0.25 to 0.25
Outputs:
- update: bfloat16 [512, 128, 8, 512], P(('replica', 'inline', 'window')), parts along dimension 0
The draws below stay inside these ranges and needn't reach their ends.
There are 4 independent parts, one for each index of `replica`. The reference program is written for one: setup_inputs(seed, part) draws one part's arguments, and reference() takes and returns one part's arrays. A program takes and returns all parts, laid end to end along the dimension named above; an argument that names none is the same for every part. Nothing has to cross between parts.
All inputs are finite; a program needn't handle non-finite values.
Results may differ from the reference program's by a relative error of at most 0.012.
The reference program's roundings to bfloat16 on the way count: a program that leaves them out, or rounds other values in their place, can miss the bound.
Values may be sent and summed in bfloat16 or wider, within the bound.
No kernel may reach another device: no remote copies, remote signals or barrier semaphores. Data moves between devices by JAX's collectives and lax.ppermute only.
A program may use at most 64 MiB of HBM per device.

```python
import jax
import jax.numpy as jnp
from jax import lax

EMBED_SPAN = 512
FOCUS_GROUPS = 16
WIN = 8
XL = 128
DEP = 8
INL = 128
TILE_TOTAL = 256


def draw_probe_match_payload_matrix(key, part):
    first, second, third = jax.random.split(jax.random.fold_in(key, 7), 3)
    width = EMBED_SPAN
    payload_vectors = jax.random.normal(third, (width, width), jnp.float32) / jnp.sqrt(1.0 * width)
    question_arrays = jax.random.normal(first, (width, width), jnp.float32) * (1.5 / jnp.sqrt(1.0 * width))
    lookup_arrays = jax.random.normal(second, (width, width), jnp.float32) * (1.5 / jnp.sqrt(1.0 * width))
    joined = jnp.concatenate([question_arrays, lookup_arrays, payload_vectors], axis=1)
    return jnp.clip(joined, -1.5, 1.5).astype(jnp.bfloat16)


def shard_levels(rng, dims, pieces, least, top_value):
    loudness = 1.0
    for axis_at, shards_of in pieces:
        draws = jax.random.uniform(jax.random.fold_in(jax.random.fold_in(rng, 6), axis_at), (shards_of,), jnp.float32, least / len(pieces), top_value / len(pieces))
        loudness = loudness * jnp.repeat(jnp.exp(draws), dims[axis_at] // shards_of).reshape((-1,) + (1,) * (len(dims) - 1 - axis_at))
    return loudness


def centred(stream_key, dims, scale, most, pieces=(), kind=jnp.bfloat16):
    values = scale * jax.random.normal(stream_key, dims, jnp.float32)
    if pieces:
        values = values * shard_levels(stream_key, dims, pieces, -0.22, 0.18)
    return jnp.clip(values, -most, most).astype(kind)


def setup_inputs(seed: int = 0, part: int = 0) -> dict:
    seeds = jax.random.split(jax.random.key(seed), 4)
    own_keys = jax.random.split(jax.random.fold_in(seeds[3], part), 4)
    return {
        "tokens": centred(own_keys[0], (INL, XL, DEP, EMBED_SPAN), 1.0, 6.0, ((0, 128),)),
        "probe_match_payload_matrix": draw_probe_match_payload_matrix(jax.random.fold_in(seeds[3], 71), part),
        "w_out": centred(seeds[2], (EMBED_SPAN, EMBED_SPAN), EMBED_SPAN ** -0.5, 0.25),
    }


EPSILON = 1e-05

def standardize_features(payload_vectors):
    center = payload_vectors - lax.optimization_barrier(jnp.mean(payload_vectors, axis=-1, keepdims=True))
    spread = lax.optimization_barrier(jnp.mean(center * center, axis=-1, keepdims=True))
    return center * lax.rsqrt(spread + EPSILON)

def round_trip(payload_vectors):
    return lax.optimization_barrier(payload_vectors.astype(jnp.bfloat16)).astype(jnp.float32)

def to_windows(block):
    first, second, third, width = block.shape
    shaped = block.reshape(first // WIN, WIN, second // WIN, WIN, third // WIN, WIN, width)
    return shaped.transpose(0, 2, 4, 1, 3, 5, 6).reshape(-1, WIN * WIN * WIN, width)

def from_windows(cube_rows, first, second, third):
    width = cube_rows.shape[-1]
    shaped = cube_rows.reshape(first // WIN, second // WIN, third // WIN, WIN, WIN, WIN, width)
    return shaped.transpose(0, 3, 1, 4, 2, 5, 6).reshape(first, second, third, width)

def tile_mixing(tile_items, probe_match_payload_matrix, digest_match_list, digest_payload_list, broad_contribution):
    count = tile_items.shape[0]
    reduced_dimension = EMBED_SPAN // FOCUS_GROUPS
    softmax_sharpness = reduced_dimension ** (-0.5)
    projected = jnp.dot(tile_items, probe_match_payload_matrix, preferred_element_type=jnp.float32).astype(jnp.bfloat16)
    question_arrays = projected[:, :EMBED_SPAN].reshape(count, FOCUS_GROUPS, reduced_dimension).astype(jnp.float32)
    lookup_arrays = projected[:, EMBED_SPAN:2 * EMBED_SPAN].reshape(count, FOCUS_GROUPS, reduced_dimension).astype(jnp.float32)
    payload_vectors = projected[:, 2 * EMBED_SPAN:].reshape(count, FOCUS_GROUPS, reduced_dimension).astype(jnp.float32)
    lookup_condensed = digest_match_list.reshape(FOCUS_GROUPS, reduced_dimension).astype(jnp.float32)
    payload_digest = digest_payload_list.reshape(FOCUS_GROUPS, reduced_dimension).astype(jnp.float32)
    per_group = FOCUS_GROUPS // 4
    results = []
    for head_group in range(4):
        bottom_bound = head_group * per_group
        ceiling_bound = bottom_bound + per_group
        similarity_raw_scores = jnp.einsum('xjr,ijr->jxi', question_arrays[:, bottom_bound:ceiling_bound], lookup_arrays[:, bottom_bound:ceiling_bound]) * softmax_sharpness
        courier_marks = jnp.einsum('yoc,oc->oy', question_arrays[:, bottom_bound:ceiling_bound], lookup_condensed[bottom_bound:ceiling_bound]) * softmax_sharpness
        top = jnp.maximum(lax.optimization_barrier(jnp.max(similarity_raw_scores, axis=-1)), courier_marks)
        weights = jnp.exp(similarity_raw_scores - top[..., None])
        car_weights = jnp.exp(courier_marks - top)
        total = lax.optimization_barrier(jnp.sum(weights, axis=-1)) + car_weights
        summed = jnp.einsum('hqk,khd->qhd', round_trip(weights), payload_vectors[:, bottom_bound:ceiling_bound])
        summed = summed + round_trip(car_weights).T[:, :, None] * payload_digest[bottom_bound:ceiling_bound][None, :, :]
        results.append(summed / total.T[:, :, None])
    local = jnp.concatenate(results, axis=1).reshape(count, EMBED_SPAN)
    return (local + broad_contribution[None, :]).astype(jnp.bfloat16)

def reference(tokens, probe_match_payload_matrix, w_out):
    reduced_dimension = EMBED_SPAN // FOCUS_GROUPS
    softmax_sharpness = reduced_dimension ** (-0.5)
    normed = standardize_features(tokens.astype(jnp.float32)).astype(jnp.bfloat16)
    tile_entries = to_windows(normed)
    averaged_tiles = lax.optimization_barrier(jnp.mean(tile_entries.astype(jnp.float32), axis=1))
    digest_items = standardize_features(averaged_tiles).astype(jnp.bfloat16)
    digest_mapping = jnp.dot(digest_items, probe_match_payload_matrix, preferred_element_type=jnp.float32).astype(jnp.bfloat16)
    condensed_question_series = digest_mapping[:, :EMBED_SPAN].reshape(TILE_TOTAL, FOCUS_GROUPS, reduced_dimension).astype(jnp.float32)
    digest_match_list = digest_mapping[:, EMBED_SPAN:2 * EMBED_SPAN]
    digest_payload_list = digest_mapping[:, 2 * EMBED_SPAN:]
    lookup_divided = digest_match_list.reshape(TILE_TOTAL, FOCUS_GROUPS, reduced_dimension).astype(jnp.float32)
    payload_split = digest_payload_list.reshape(TILE_TOTAL, FOCUS_GROUPS, reduced_dimension).astype(jnp.float32)
    similarity_raw_scores = jnp.einsum('xjr,ijr->jxi', condensed_question_series, lookup_divided) * softmax_sharpness
    top = lax.optimization_barrier(jnp.max(similarity_raw_scores, axis=-1, keepdims=True))
    weights = jnp.exp(similarity_raw_scores - top)
    total = lax.optimization_barrier(jnp.sum(weights, axis=-1))
    summed = jnp.einsum('hqk,khd->qhd', round_trip(weights), payload_split)
    broad_context = (summed / total.T[:, :, None]).reshape(TILE_TOTAL, EMBED_SPAN)

    def single_tile(window_item):
        nested_step = tile_mixing(window_item[0], probe_match_payload_matrix, window_item[1], window_item[2], window_item[3])
        return jnp.dot(nested_step, w_out, preferred_element_type=jnp.float32).astype(jnp.bfloat16)
    increments = lax.map(single_tile, (tile_entries, digest_match_list, digest_payload_list, broad_context))
    return from_windows(increments, INL, XL, DEP)
```

```python
import jax
import jax.numpy as jnp
from jax import lax
from jax.experimental import pallas as pl
from jax.experimental.pallas import tpu as pltpu
from jax.sharding import PartitionSpec as P

EMBED_SPAN = 512
HEADS = 16
HEAD_DIM = EMBED_SPAN // HEADS
WIN = 8
EPSILON = 1e-05
LOG2E = 1.4426950408889634
SCALE = HEAD_DIM ** (-0.5)
F32 = jnp.float32
BF16 = jnp.bfloat16
VMEM_LIMIT = 48 * 1024 * 1024


def standardize(values):
    center = values - jnp.mean(values, axis=-1, keepdims=True)
    spread = jnp.mean(center * center, axis=-1, keepdims=True)
    return center * lax.rsqrt(spread + EPSILON)


def norm_kernel(x_ref, normed_ref, sums_ref):
    dests, tokens, width = x_ref.shape
    normed = standardize(x_ref[...].astype(F32)).astype(BF16)
    normed_ref[...] = normed
    cells = normed.astype(F32).reshape(dests * tokens // (WIN * WIN), WIN * WIN, width)
    sums_ref[...] = jnp.sum(cells, axis=1)


def carrier_kernel(sums_ref, out_ref):
    total = jnp.sum(sums_ref[...], axis=1)
    out_ref[...] = standardize(total * (1.0 / WIN**3)).astype(BF16).reshape(out_ref.shape)


def head_mask(rows):
    lane = lax.broadcasted_iota(jnp.int32, (rows, EMBED_SPAN), 1) // HEAD_DIM
    row = lax.broadcasted_iota(jnp.int32, (rows, EMBED_SPAN), 0) % HEADS
    return lane == row


def glob_kernel(all_ref, own_ref, w_ref, out_ref):
    own_count = own_ref.shape[0]
    match = jnp.dot(all_ref[...], w_ref[:, EMBED_SPAN:], preferred_element_type=F32).astype(BF16)
    keys, values = match[:, :EMBED_SPAN], match[:, EMBED_SPAN:]
    own = jnp.concatenate([own_ref[...].astype(F32), jnp.zeros((16 - own_count, EMBED_SPAN), F32)], axis=0).astype(BF16)
    proj = jnp.dot(own, w_ref[...], preferred_element_type=F32).astype(BF16).astype(F32)
    mask = head_mask(HEADS)
    for c in range(own_count):
        row = proj[c : c + 1]
        queries = jnp.where(mask, row[:, :EMBED_SPAN], 0.0).astype(BF16)
        s = lax.dot_general(queries, keys, (((1,), (1,)), ((), ())), preferred_element_type=F32) * SCALE
        weights = jnp.exp(s - jnp.max(s, axis=-1, keepdims=True))
        total = jnp.sum(weights, axis=-1, keepdims=True)
        summed = jnp.dot(weights.astype(BF16), values, preferred_element_type=F32) / total
        glob = jnp.sum(jnp.where(mask, summed, 0.0), axis=0, keepdims=True)
        out_ref[c] = jnp.concatenate(
            [glob, row[:, EMBED_SPAN : 2 * EMBED_SPAN], row[:, 2 * EMBED_SPAN :], jnp.zeros((5, EMBED_SPAN), F32)], axis=0
        )


def window_kernel(x_ref, aux_ref, wk_ref, wqt_ref, wvt_ref, wo_ref, out_ref, k_s, qh_s, ql_s, vt_s, sc_s, vc_s, gl_s, inner_s):
    count = WIN**3
    x = x_ref[...].reshape(count, EMBED_SPAN)
    nt = (((1,), (1,)), ((), ()))
    k_s[...] = jnp.dot(x, wk_ref[...], preferred_element_type=F32).astype(BF16)
    q = lax.dot_general(wqt_ref[...], x, nt, preferred_element_type=F32).astype(BF16).astype(F32) * (SCALE * LOG2E)
    high = q.astype(BF16)
    low = (q - high.astype(F32)).astype(BF16)
    qh_s[...] = high
    ql_s[...] = low
    vt_s[...] = lax.dot_general(wvt_ref[...], x, nt, preferred_element_type=F32).astype(BF16)
    aux = aux_ref[0]
    kc = jnp.where(head_mask(HEADS), aux[1:2], 0.0).astype(BF16)
    sc_s[...] = jnp.dot(kc, high, preferred_element_type=F32) + jnp.dot(kc, low, preferred_element_type=F32)
    gl_s[...] = jnp.broadcast_to(aux[0:1], (128, EMBED_SPAN)).T
    vc_s[...] = jnp.broadcast_to(aux[2:3], (128, EMBED_SPAN)).T
    ones = jnp.ones((16, count), BF16)

    def widen(column):
        return jnp.concatenate([column] * (count // 128), axis=1)

    def group(g, carry):
        lanes = pl.ds(pl.multiple_of(g * 128, 128), 128)
        kg = k_s[:, lanes]
        kk = jnp.concatenate([kg, kg], axis=1)
        for j in range(4):
            h = g * 4 + j
            rows = pl.ds(pl.multiple_of(h * HEAD_DIM, HEAD_DIM), HEAD_DIM)

            def place(part):
                pieces = []
                if j:
                    pieces.append(jnp.zeros((HEAD_DIM * j, count), BF16))
                pieces.append(part)
                if j < 3:
                    pieces.append(jnp.zeros((HEAD_DIM * (3 - j), count), BF16))
                return pieces

            qq = jnp.concatenate(place(qh_s[rows, :]) + place(ql_s[rows, :]), axis=0)
            s = jnp.dot(kk, qq, preferred_element_type=F32)
            sc = sc_s[pl.ds(h, 1), :]
            top = jnp.maximum(jnp.max(s, axis=0, keepdims=True), sc)
            weights = jnp.exp2(s - top).astype(BF16)
            pc = jnp.exp2(sc - top)
            vv = jnp.concatenate([vt_s[rows, :], ones], axis=0)
            o = jnp.dot(vv, weights, preferred_element_type=F32)
            total = o[HEAD_DIM : HEAD_DIM + 1] + pc
            summed = o[:HEAD_DIM] + widen(vc_s[rows, :]) * pc.astype(BF16).astype(F32)
            inner_s[rows, :] = (summed / total + widen(gl_s[rows, :])).astype(BF16)
        return carry

    lax.fori_loop(0, HEADS // 4, group, 0)
    tn = (((0,), (0,)), ((), ()))
    update = lax.dot_general(inner_s[...], wo_ref[...], tn, preferred_element_type=F32)
    out_ref[...] = update.astype(BF16).reshape(out_ref.shape)


def window_attention(grouped, aux, wk, wqt, wvt, wo):
    rows, tokens, width = grouped.shape
    cell = WIN * WIN
    count = rows * cell
    whole = pl.BlockSpec((width, width), lambda c: (0, 0))
    cube = pl.BlockSpec((rows, cell, width), lambda c: (0, c, 0))
    return pl.pallas_call(
        window_kernel,
        grid=(tokens // cell,),
        in_specs=[cube, pl.BlockSpec((1, 8, width), lambda c: (c, 0, 0)), whole, whole, whole, whole],
        out_specs=cube,
        out_shape=jax.ShapeDtypeStruct(grouped.shape, BF16),
        scratch_shapes=[
            pltpu.VMEM((count, width), BF16),
            pltpu.VMEM((width, count), BF16),
            pltpu.VMEM((width, count), BF16),
            pltpu.VMEM((width, count), BF16),
            pltpu.VMEM((HEADS, count), F32),
            pltpu.VMEM((width, 128), F32),
            pltpu.VMEM((width, 128), F32),
            pltpu.VMEM((width, count), BF16),
        ],
        compiler_params=pltpu.CompilerParams(vmem_limit_bytes=VMEM_LIMIT),
        cost_estimate=pl.CostEstimate(flops=20_000_000_000, bytes_accessed=4 << 20, transcendentals=8 << 20),
    )(grouped, aux, wk, wqt, wvt, wo)


def normalize(rows):
    dests, tokens, width = rows.shape
    steps = 2
    cells = dests * tokens // (WIN * WIN)
    return pl.pallas_call(
        norm_kernel,
        grid=(steps,),
        in_specs=[pl.BlockSpec((dests // steps, tokens, width), lambda i: (i, 0, 0))],
        out_specs=[
            pl.BlockSpec((dests // steps, tokens, width), lambda i: (i, 0, 0)),
            pl.BlockSpec((cells // steps, width), lambda i: (i, 0)),
        ],
        out_shape=[
            jax.ShapeDtypeStruct(rows.shape, BF16),
            jax.ShapeDtypeStruct((cells, width), F32),
        ],
        compiler_params=pltpu.CompilerParams(vmem_limit_bytes=VMEM_LIMIT),
        cost_estimate=pl.CostEstimate(flops=10_000_000, bytes_accessed=2 << 20, transcendentals=0),
    )(rows)


def carrier_tokens(sums):
    halves, rows, cells, width = sums.shape
    return pl.pallas_call(
        carrier_kernel,
        out_shape=jax.ShapeDtypeStruct((halves * cells, width), BF16),
        compiler_params=pltpu.CompilerParams(vmem_limit_bytes=VMEM_LIMIT),
        cost_estimate=pl.CostEstimate(flops=1_000_000, bytes_accessed=1 << 19, transcendentals=0),
    )(sums)


def glob_of(carriers, own, weights):
    return pl.pallas_call(
        glob_kernel,
        out_shape=jax.ShapeDtypeStruct((own.shape[0], 8, own.shape[1]), F32),
        compiler_params=pltpu.CompilerParams(vmem_limit_bytes=VMEM_LIMIT),
        cost_estimate=pl.CostEstimate(flops=300_000_000, bytes_accessed=2 << 20, transcendentals=16384),
    )(carriers, own, weights)


def body(tokens, weights, w_out):
    window = lax.axis_size("window")
    width = tokens.shape[-1]
    groups = [[h * WIN + l for l in range(WIN)] for h in range(window // WIN)]
    rows = tokens.reshape(WIN, -1, width)
    own_count = rows.shape[1] // (WIN * WIN)
    normed, sums = normalize(rows)
    grouped = lax.all_to_all(normed, "window", split_axis=0, concat_axis=0, tiled=True, axis_index_groups=groups)
    sums = lax.all_gather(sums, "window", axis=0)
    near = carrier_tokens(sums.reshape(window // WIN, WIN, sums.shape[1], width))
    own = lax.dynamic_slice_in_dim(near, lax.axis_index("window") * own_count, own_count, 0)
    carriers = lax.all_gather(near, "inline", axis=0, tiled=True)
    aux = glob_of(carriers, own, weights)
    wqt = weights[:, :EMBED_SPAN].T
    wk = weights[:, EMBED_SPAN : 2 * EMBED_SPAN]
    wvt = weights[:, 2 * EMBED_SPAN :].T
    update = window_attention(grouped, aux, wk, wqt, wvt, w_out)
    returned = lax.all_to_all(update, "window", split_axis=0, concat_axis=0, tiled=True, axis_index_groups=groups)
    return returned.reshape(tokens.shape)


def solution(mesh):
    return jax.shard_map(
        body,
        mesh=mesh,
        in_specs=(P(("replica", "inline", "window"), None, None, None), P(), P()),
        out_specs=P(("replica", "inline", "window"), None, None, None),
        check_vma=False,
    )
```

```python
import jax
import jax.numpy as jnp
from jax import lax
from jax.experimental import pallas as pl
from jax.experimental.pallas import tpu as pltpu
from jax.sharding import PartitionSpec as P

EMBED_SPAN = 512
HEADS = 16
HEAD_DIM = EMBED_SPAN // HEADS
WIN = 8
EPSILON = 1e-05
LOG2E = 1.4426950408889634
SCALE = HEAD_DIM ** (-0.5)
F32 = jnp.float32
BF16 = jnp.bfloat16
NT = (((1,), (1,)), ((), ()))
TN = (((0,), (0,)), ((), ()))
PARAMS = pltpu.CompilerParams(vmem_limit_bytes=32 * 1024 * 1024)


def cost(flops, size, transcendentals=0):
    return pl.CostEstimate(flops=flops, bytes_accessed=size, transcendentals=transcendentals)


def in_hbm(*arrays):
    return [pltpu.with_memory_space_constraint(a, pltpu.HBM) for a in arrays]


def standardize(values):
    center = values - jnp.mean(values, axis=-1, keepdims=True)
    spread = jnp.mean(center * center, axis=-1, keepdims=True)
    return center * lax.rsqrt(spread + EPSILON)


def norm_kernel(x_ref, wq_ref, wv_ref, normed_ref, wqt_ref, wvt_ref):
    normed_ref[...] = standardize(x_ref[...].astype(F32)).astype(BF16)

    @pl.when(pl.program_id(0) == 0)
    def _():
        row = lax.broadcasted_iota(jnp.int32, (EMBED_SPAN, EMBED_SPAN), 0)
        lane = lax.broadcasted_iota(jnp.int32, (EMBED_SPAN, EMBED_SPAN), 1)
        eye = jnp.where(row == lane, 1.0, 0.0).astype(BF16)
        wqt_ref[...] = lax.dot_general(eye, wq_ref[...], NT, preferred_element_type=F32).astype(BF16)
        wvt_ref[...] = lax.dot_general(eye, wv_ref[...], NT, preferred_element_type=F32).astype(BF16)


def normalize(rows, weights):
    dests, tokens, width = rows.shape
    steps = 4
    block = pl.BlockSpec((dests // steps, tokens, width), lambda i: (i, 0, 0))
    square = pltpu.HBM((width, width), BF16)
    whole = pl.BlockSpec((width, width), lambda i: (0, 0))
    rows, weights = in_hbm(rows, weights)
    return pl.pallas_call(
        norm_kernel,
        grid=(steps,),
        in_specs=[block, whole, pl.BlockSpec((width, width), lambda i: (0, 2))],
        out_specs=[block, whole, whole],
        out_shape=[jax.ShapeDtypeStruct(rows.shape, BF16), square, square],
        compiler_params=PARAMS,
        cost_estimate=cost(600_000_000, 4 << 20),
    )(rows, weights, weights)


def carrier_kernel(x_ref, out_ref, copies_ref):
    rows, tokens, width = x_ref.shape
    cell = WIN * WIN
    own = []
    for c in range(tokens // cell):
        cube = x_ref[:, c * cell : (c + 1) * cell, :].astype(F32)
        mean = jnp.sum(jnp.sum(cube, axis=0), axis=0, keepdims=True) * (1.0 / (rows * cell))
        own.append(standardize(mean))
        out_ref[c] = jnp.broadcast_to(own[-1].astype(BF16).astype(F32), (8, width))
    copies_ref[...] = jnp.broadcast_to(jnp.concatenate(own, axis=0)[None], copies_ref.shape).astype(BF16)


def own_carriers(grouped, window):
    rows, tokens, width = grouped.shape
    own_count = tokens // (WIN * WIN)
    return pl.pallas_call(
        carrier_kernel,
        out_shape=[jax.ShapeDtypeStruct((own_count, 8, width), F32), jax.ShapeDtypeStruct((window, own_count, width), BF16)],
        compiler_params=PARAMS,
        cost_estimate=cost(1_000_000, 1 << 20),
    )(grouped)


def head_mask(rows):
    lane = lax.broadcasted_iota(jnp.int32, (rows, EMBED_SPAN), 1) // HEAD_DIM
    row = lax.broadcasted_iota(jnp.int32, (rows, EMBED_SPAN), 0) % HEADS
    return lane == row


def window_kernel(x_ref, car_ref, wk_ref, wqt_ref, wvt_ref, out_ref, k_s, qh_s, ql_s, vt_s, sc_s, vc_s):
    count = WIN**3
    x = x_ref[...].reshape(count, EMBED_SPAN)
    k_s[...] = jnp.dot(x, wk_ref[...], preferred_element_type=F32).astype(BF16)
    q = lax.dot_general(wqt_ref[...], x, NT, preferred_element_type=F32).astype(BF16).astype(F32) * (SCALE * LOG2E)
    high = q.astype(BF16)
    low = (q - high.astype(F32)).astype(BF16)
    qh_s[...] = high
    ql_s[...] = low
    vt_s[...] = lax.dot_general(wvt_ref[...], x, NT, preferred_element_type=F32).astype(BF16)
    carrier = jnp.broadcast_to(car_ref[0, 0:1, :], (128, EMBED_SPAN)).astype(BF16)
    kc = jnp.dot(carrier[:16], wk_ref[...], preferred_element_type=F32)
    kc = jnp.where(head_mask(HEADS), kc, 0.0).astype(BF16)
    sc_s[...] = jnp.dot(kc, high, preferred_element_type=F32) + jnp.dot(kc, low, preferred_element_type=F32)
    vc_s[...] = lax.dot_general(wvt_ref[...], carrier, NT, preferred_element_type=F32).astype(BF16).astype(F32)
    ones = jnp.ones((16, count), BF16)

    def scores(h):
        group, j = h // 4, h % 4
        keys = k_s[:, group * 128 : (group + 1) * 128]
        rows = slice(h * HEAD_DIM, (h + 1) * HEAD_DIM)
        before = [jnp.zeros((HEAD_DIM * j, count), BF16)] if j else []
        after = [jnp.zeros((HEAD_DIM * (3 - j), count), BF16)] if j < 3 else []
        queries = before + [qh_s[rows, :]] + after + before + [ql_s[rows, :]] + after
        return jnp.dot(jnp.concatenate([keys, keys], axis=1), jnp.concatenate(queries, axis=0), preferred_element_type=F32)

    def mix(h, s):
        rows = slice(h * HEAD_DIM, (h + 1) * HEAD_DIM)
        sc = sc_s[h : h + 1, :]
        top = jnp.maximum(jnp.max(s, axis=0, keepdims=True), sc)
        weights = jnp.exp2(s - top).astype(BF16)
        pc = jnp.exp2(sc - top)
        values = jnp.concatenate([vt_s[rows, :], ones], axis=0)
        o = jnp.dot(values, weights, preferred_element_type=F32)
        total = o[HEAD_DIM : HEAD_DIM + 1] + pc
        column = jnp.concatenate([vc_s[rows, :]] * (count // 128), axis=1)
        out_ref[rows, :] = (o[:HEAD_DIM] + column * pc.astype(BF16).astype(F32)) / total

    ahead = []
    for h in range(HEADS):
        ahead.append((h, scores(h)))
        if len(ahead) > 2:
            mix(*ahead.pop(0))
    for item in ahead:
        mix(*item)


def window_attention(grouped, own, c, weights, wqt, wvt):
    rows, tokens, width = grouped.shape
    cell = WIN * WIN
    count = rows * cell
    whole = pl.BlockSpec((width, width), lambda i: (0, 0))
    half = pltpu.VMEM((width, count), BF16)
    weights, wqt, wvt = in_hbm(weights, wqt, wvt)
    return pl.pallas_call(
        window_kernel,
        grid=(1,),
        in_specs=[
            pl.BlockSpec((rows, cell, width), lambda i: (0, c, 0)),
            pl.BlockSpec((1, 8, width), lambda i: (c, 0, 0)),
            pl.BlockSpec((width, width), lambda i: (0, 1)),
            whole,
            whole,
        ],
        out_specs=pl.BlockSpec((width, count), lambda i: (0, 0)),
        out_shape=pltpu.HBM((width, count), F32),
        scratch_shapes=[pltpu.VMEM((count, width), BF16), half, half, half, pltpu.VMEM((HEADS, count), F32), pltpu.VMEM((width, 128), F32)],
        compiler_params=PARAMS,
        cost_estimate=cost(8_000_000_000, 4 << 20, 4 << 20),
    )(grouped, own, weights, wqt, wvt)


def glob_kernel(all_ref, own_ref, w_ref, wo_ref, *rest):
    out_ref = rest[-1]
    match = jnp.dot(all_ref[...], w_ref[:, EMBED_SPAN:], preferred_element_type=F32).astype(BF16)
    keys, values = match[:, :EMBED_SPAN], match[:, EMBED_SPAN:]
    mask = head_mask(HEADS)
    cell = WIN * WIN
    for c, local_ref in enumerate(rest[:-1]):
        own = jnp.broadcast_to(own_ref[c, 0:1, :], (16, EMBED_SPAN)).astype(BF16)
        queries = jnp.dot(own, w_ref[:, :EMBED_SPAN], preferred_element_type=F32)
        queries = jnp.where(mask, queries, 0.0).astype(BF16)
        s = lax.dot_general(queries, keys, NT, preferred_element_type=F32) * SCALE
        weights = jnp.exp(s - jnp.max(s, axis=-1, keepdims=True))
        total = jnp.sum(weights, axis=-1, keepdims=True)
        summed = jnp.dot(weights.astype(BF16), values, preferred_element_type=F32) / total
        glob = jnp.sum(jnp.where(mask, summed, 0.0), axis=0, keepdims=True)
        column = jnp.broadcast_to(glob, (128, EMBED_SPAN)).T
        column = jnp.concatenate([column] * (local_ref.shape[1] // 128), axis=1)
        inner = (local_ref[...] + column).astype(BF16)
        update = lax.dot_general(inner, wo_ref[...], TN, preferred_element_type=F32).astype(BF16)
        out_ref[:, c * cell : (c + 1) * cell, :] = update.reshape(-1, cell, EMBED_SPAN)


def finish(carriers, own, weights, w_out, local, shape):
    return pl.pallas_call(
        glob_kernel,
        out_shape=jax.ShapeDtypeStruct(shape, BF16),
        compiler_params=PARAMS,
        cost_estimate=cost(1_000_000_000, 6 << 20, 16384),
    )(carriers, own, weights, w_out, *in_hbm(*local))


def exchange(values, axis, groups=None):
    return lax.all_to_all(values, axis, split_axis=0, concat_axis=0, tiled=True, axis_index_groups=groups)


def spread(values, axis):
    return exchange(jnp.broadcast_to(values[None], (lax.axis_size(axis),) + values.shape), axis)


def body(tokens, weights, w_out):
    window = lax.axis_size("window")
    width = tokens.shape[-1]
    groups = [[h * WIN + l for l in range(WIN)] for h in range(window // WIN)]
    rows = tokens.reshape(WIN, -1, width)
    normed, wqt, wvt = normalize(rows, weights)
    grouped = exchange(normed, "window", groups)
    own, copies = own_carriers(grouped, window)
    near = exchange(copies, "window").reshape(-1, width)
    first = window_attention(grouped, own, 0, weights, wqt, wvt)
    grouped, near = lax.optimization_barrier((grouped, near))
    carriers = spread(near, "inline").reshape(-1, width)
    second = window_attention(grouped, own, 1, weights, wqt, wvt)
    update = finish(carriers, own, weights, w_out, (first, second), grouped.shape)
    return exchange(update, "window", groups).reshape(tokens.shape)


def solution(mesh):
    return jax.shard_map(
        body,
        mesh=mesh,
        in_specs=(P(("replica", "inline", "window"), None, None, None), P(), P()),
        out_specs=P(("replica", "inline", "window"), None, None, None),
        check_vma=False,
    )
```

```python
import jax
import jax.numpy as jnp
from jax import lax
from jax.experimental import pallas as pl
from jax.experimental.pallas import tpu as pltpu
from jax.sharding import PartitionSpec as P

EMBED_SPAN = 512
HEADS = 16
HEAD_DIM = EMBED_SPAN // HEADS
WIN = 8
EPSILON = 1e-05
LOG2E = 1.4426950408889634
SCALE = HEAD_DIM ** (-0.5)
F32 = jnp.float32
BF16 = jnp.bfloat16
NT = (((1,), (1,)), ((), ()))
TN = (((0,), (0,)), ((), ()))
PARAMS = pltpu.CompilerParams(vmem_limit_bytes=32 * 1024 * 1024)


def cost(flops, size, transcendentals=0):
    return pl.CostEstimate(flops=flops, bytes_accessed=size, transcendentals=transcendentals)


def in_hbm(*arrays):
    return [pltpu.with_memory_space_constraint(a, pltpu.HBM) for a in arrays]


def standardize(values):
    center = values - jnp.mean(values, axis=-1, keepdims=True)
    spread = jnp.mean(center * center, axis=-1, keepdims=True)
    return center * lax.rsqrt(spread + EPSILON)


def norm_kernel(x_ref, normed_ref, sums_ref):
    dests, tokens, width = x_ref.shape
    cell = WIN * WIN
    normed = standardize(x_ref[...].astype(F32)).astype(BF16)
    normed_ref[...] = normed
    sums_ref[...] = jnp.sum(normed.astype(F32).reshape(dests, tokens // cell, cell, width), axis=2)


def normalize(rows):
    dests, tokens, width = rows.shape
    steps = 4
    cells = tokens // (WIN * WIN)
    block = pl.BlockSpec((dests // steps, tokens, width), lambda i: (i, 0, 0))
    return pl.pallas_call(
        norm_kernel,
        grid=(steps,),
        in_specs=[block],
        out_specs=[block, pl.BlockSpec((dests // steps, cells, width), lambda i: (i, 0, 0))],
        out_shape=[jax.ShapeDtypeStruct(rows.shape, BF16), jax.ShapeDtypeStruct((dests, cells, width), F32)],
        compiler_params=PARAMS,
        cost_estimate=cost(10_000_000, 2 << 20),
    )(*in_hbm(rows))


def turn_kernel(wq_ref, wv_ref, wqt_ref, wvt_ref):
    row = lax.broadcasted_iota(jnp.int32, (EMBED_SPAN, EMBED_SPAN), 0)
    lane = lax.broadcasted_iota(jnp.int32, (EMBED_SPAN, EMBED_SPAN), 1)
    eye = jnp.where(row == lane, 1.0, 0.0).astype(BF16)
    wqt_ref[...] = lax.dot_general(eye, wq_ref[...], NT, preferred_element_type=F32).astype(BF16)
    wvt_ref[...] = lax.dot_general(eye, wv_ref[...], NT, preferred_element_type=F32).astype(BF16)


def turn(weights):
    width = weights.shape[0]
    square = pltpu.HBM((width, width), BF16)
    whole = pl.BlockSpec((width, width), lambda i: (0, 0))
    (weights,) = in_hbm(weights)
    return pl.pallas_call(
        turn_kernel,
        grid=(1,),
        in_specs=[whole, pl.BlockSpec((width, width), lambda i: (0, 2))],
        out_specs=[whole, whole],
        out_shape=[square, square],
        compiler_params=PARAMS,
        cost_estimate=cost(600_000_000, 2 << 20),
    )(weights, weights)


def carrier_kernel(x_ref, out_ref, copies_ref):
    own_count, rows, width = out_ref.shape
    tokens = x_ref.shape[1] // own_count
    own = []
    for c in range(own_count):
        cube = x_ref[:, c * tokens : (c + 1) * tokens, :].astype(F32)
        mean = jnp.sum(jnp.sum(cube, axis=0), axis=0, keepdims=True) * (1.0 / WIN**3)
        own.append(standardize(mean))
        out_ref[c] = jnp.broadcast_to(own[-1].astype(BF16).astype(F32), (rows, width))
    copies_ref[...] = jnp.broadcast_to(jnp.concatenate(own, axis=0)[None], copies_ref.shape).astype(BF16)


def own_carriers(values, own_count, window):
    width = values.shape[-1]
    return pl.pallas_call(
        carrier_kernel,
        out_shape=[jax.ShapeDtypeStruct((own_count, 8, width), F32), jax.ShapeDtypeStruct((window, own_count, width), BF16)],
        compiler_params=PARAMS,
        cost_estimate=cost(1_000_000, 1 << 20),
    )(values)


def head_mask(rows):
    lane = lax.broadcasted_iota(jnp.int32, (rows, EMBED_SPAN), 1) // HEAD_DIM
    row = lax.broadcasted_iota(jnp.int32, (rows, EMBED_SPAN), 0) % HEADS
    return lane == row


def widen(column, count):
    return jnp.concatenate([column] * (count // 128), axis=1)


def attend(x_ref, car_ref, wk_ref, wqt_ref, wvt_ref, k_s, qh_s, ql_s, vt_s, sc_s, vc_s, write):
    count = WIN**3
    x = x_ref[...].reshape(count, EMBED_SPAN)
    k_s[...] = jnp.dot(x, wk_ref[...], preferred_element_type=F32).astype(BF16)
    q = lax.dot_general(wqt_ref[...], x, NT, preferred_element_type=F32).astype(BF16).astype(F32) * (SCALE * LOG2E)
    high = q.astype(BF16)
    low = (q - high.astype(F32)).astype(BF16)
    qh_s[...] = high
    ql_s[...] = low
    vt_s[...] = lax.dot_general(wvt_ref[...], x, NT, preferred_element_type=F32).astype(BF16)
    carrier = jnp.broadcast_to(car_ref[0, 0:1, :], (128, EMBED_SPAN)).astype(BF16)
    kc = jnp.dot(carrier[:16], wk_ref[...], preferred_element_type=F32)
    kc = jnp.where(head_mask(HEADS), kc, 0.0).astype(BF16)
    sc_s[...] = jnp.dot(kc, high, preferred_element_type=F32) + jnp.dot(kc, low, preferred_element_type=F32)
    vc_s[...] = lax.dot_general(wvt_ref[...], carrier, NT, preferred_element_type=F32).astype(BF16).astype(F32)
    ones = jnp.ones((16, count), BF16)

    def scores(h):
        group, j = h // 4, h % 4
        keys = k_s[:, group * 128 : (group + 1) * 128]
        rows = slice(h * HEAD_DIM, (h + 1) * HEAD_DIM)
        before = [jnp.zeros((HEAD_DIM * j, count), BF16)] if j else []
        after = [jnp.zeros((HEAD_DIM * (3 - j), count), BF16)] if j < 3 else []
        queries = before + [qh_s[rows, :]] + after + before + [ql_s[rows, :]] + after
        return jnp.dot(jnp.concatenate([keys, keys], axis=1), jnp.concatenate(queries, axis=0), preferred_element_type=F32)

    def mix(h, s):
        rows = slice(h * HEAD_DIM, (h + 1) * HEAD_DIM)
        sc = sc_s[h : h + 1, :]
        top = jnp.maximum(jnp.max(s, axis=0, keepdims=True), sc)
        weights = jnp.exp2(s - top).astype(BF16)
        pc = jnp.exp2(sc - top)
        values = jnp.concatenate([vt_s[rows, :], ones], axis=0)
        o = jnp.dot(values, weights, preferred_element_type=F32)
        total = o[HEAD_DIM : HEAD_DIM + 1] + pc
        write(rows, (o[:HEAD_DIM] + widen(vc_s[rows, :], count) * pc.astype(BF16).astype(F32)) / total)

    ahead = []
    for h in range(HEADS):
        ahead.append((h, scores(h)))
        if len(ahead) > 2:
            mix(*ahead.pop(0))
    for item in ahead:
        mix(*item)


def attend_scratch():
    count = WIN**3
    half = pltpu.VMEM((EMBED_SPAN, count), BF16)
    return [pltpu.VMEM((count, EMBED_SPAN), BF16), half, half, half, pltpu.VMEM((HEADS, count), F32), pltpu.VMEM((EMBED_SPAN, 128), F32)]


def local_kernel(x_ref, car_ref, wk_ref, wqt_ref, wvt_ref, out_ref, *scratch):
    def write(rows, local):
        out_ref[rows, :] = local

    attend(x_ref, car_ref, wk_ref, wqt_ref, wvt_ref, *scratch, write)


def local_attention(grouped, own, c, weights, wqt, wvt):
    rows, tokens, width = grouped.shape
    cell = WIN * WIN
    count = rows * cell
    whole = pl.BlockSpec((width, width), lambda i: (0, 0))
    weights, wqt, wvt = in_hbm(weights, wqt, wvt)
    return pl.pallas_call(
        local_kernel,
        grid=(1,),
        in_specs=[
            pl.BlockSpec((rows, cell, width), lambda i: (0, c, 0)),
            pl.BlockSpec((1, 8, width), lambda i: (c, 0, 0)),
            pl.BlockSpec((width, width), lambda i: (0, 1)),
            whole,
            whole,
        ],
        out_specs=pl.BlockSpec((width, count), lambda i: (0, 0)),
        out_shape=pltpu.HBM((width, count), F32),
        scratch_shapes=attend_scratch(),
        compiler_params=PARAMS,
        cost_estimate=cost(8_000_000_000, 4 << 20, 4 << 20),
    )(grouped, own, weights, wqt, wvt)


def whole_kernel(x_ref, car_ref, glob_ref, wk_ref, wqt_ref, wvt_ref, wo_ref, out_ref, inner_s, gl_s, *scratch):
    gl_s[...] = jnp.broadcast_to(glob_ref[0, 0:1, :], (128, EMBED_SPAN)).T

    def write(rows, local):
        inner_s[rows, :] = (local + widen(gl_s[rows, :], local.shape[1])).astype(BF16)

    attend(x_ref, car_ref, wk_ref, wqt_ref, wvt_ref, *scratch, write)
    update = lax.dot_general(inner_s[...], wo_ref[...], TN, preferred_element_type=F32)
    out_ref[...] = update.astype(BF16).reshape(out_ref.shape)


def whole_attention(grouped, own, glob, weights, wqt, wvt, w_out):
    rows, tokens, width = grouped.shape
    cell = WIN * WIN
    count = rows * cell
    cube = pl.BlockSpec((rows, cell, width), lambda i: (0, i, 0))
    row = pl.BlockSpec((1, 8, width), lambda i: (i, 0, 0))
    whole = pl.BlockSpec((width, width), lambda i: (0, 0))
    return pl.pallas_call(
        whole_kernel,
        grid=(tokens // cell,),
        in_specs=[cube, row, row, pl.BlockSpec((width, width), lambda i: (0, 1)), whole, whole, whole],
        out_specs=cube,
        out_shape=jax.ShapeDtypeStruct(grouped.shape, BF16),
        scratch_shapes=[pltpu.VMEM((width, count), BF16), pltpu.VMEM((width, 128), F32)] + attend_scratch(),
        compiler_params=PARAMS,
        cost_estimate=cost(17_000_000_000, 6 << 20, 8 << 20),
    )(grouped, own, glob, *in_hbm(weights, wqt, wvt, w_out))


def carrier_match(all_ref, w_ref):
    match = jnp.dot(all_ref[...], w_ref[:, EMBED_SPAN:], preferred_element_type=F32).astype(BF16)
    return match[:, :EMBED_SPAN], match[:, EMBED_SPAN:]


def carrier_attention(own, w_ref, keys, values):
    mask = head_mask(HEADS)
    own = jnp.broadcast_to(own, (16, EMBED_SPAN)).astype(BF16)
    queries = jnp.dot(own, w_ref[:, :EMBED_SPAN], preferred_element_type=F32)
    queries = jnp.where(mask, queries, 0.0).astype(BF16)
    s = lax.dot_general(queries, keys, NT, preferred_element_type=F32) * SCALE
    weights = jnp.exp(s - jnp.max(s, axis=-1, keepdims=True))
    total = jnp.sum(weights, axis=-1, keepdims=True)
    summed = jnp.dot(weights.astype(BF16), values, preferred_element_type=F32) / total
    return jnp.sum(jnp.where(mask, summed, 0.0), axis=0, keepdims=True)


def glob_kernel(all_ref, own_ref, w_ref, out_ref):
    keys, values = carrier_match(all_ref, w_ref)
    for c in range(out_ref.shape[0]):
        out_ref[c] = jnp.broadcast_to(carrier_attention(own_ref[c, 0:1, :], w_ref, keys, values), out_ref.shape[1:])


def glob_of(carriers, own, weights):
    return pl.pallas_call(
        glob_kernel,
        out_shape=jax.ShapeDtypeStruct(own.shape, F32),
        compiler_params=PARAMS,
        cost_estimate=cost(400_000_000, 2 << 20, 16384),
    )(carriers, own, weights)


def finish_kernel(all_ref, own_ref, w_ref, wo_ref, *rest):
    out_ref = rest[-1]
    keys, values = carrier_match(all_ref, w_ref)
    cell = WIN * WIN
    for c, local_ref in enumerate(rest[:-1]):
        glob = carrier_attention(own_ref[c, 0:1, :], w_ref, keys, values)
        column = widen(jnp.broadcast_to(glob, (128, EMBED_SPAN)).T, local_ref.shape[1])
        inner = (local_ref[...] + column).astype(BF16)
        update = lax.dot_general(inner, wo_ref[...], TN, preferred_element_type=F32).astype(BF16)
        out_ref[:, c * cell : (c + 1) * cell, :] = update.reshape(-1, cell, EMBED_SPAN)


def finish(carriers, own, weights, w_out, local, shape):
    return pl.pallas_call(
        finish_kernel,
        out_shape=jax.ShapeDtypeStruct(shape, BF16),
        compiler_params=PARAMS,
        cost_estimate=cost(1_000_000_000, 6 << 20, 16384),
    )(carriers, own, weights, w_out, *in_hbm(*local))


def exchange(values, axis, groups=None):
    return lax.all_to_all(values, axis, split_axis=0, concat_axis=0, tiled=True, axis_index_groups=groups)


def spread(values, axis):
    return exchange(jnp.broadcast_to(values[None], (lax.axis_size(axis),) + values.shape), axis)


def slab_first(normed, sums, weights, w_out, groups, window):
    width = normed.shape[-1]
    grouped = exchange(normed, "window", groups)
    own, copies = own_carriers(grouped, sums.shape[1], window)
    wqt, wvt = turn(weights)
    near = exchange(copies, "window").reshape(-1, width)
    first = local_attention(grouped, own, 0, weights, wqt, wvt)
    grouped, near = lax.optimization_barrier((grouped, near))
    carriers = spread(near, "inline").reshape(-1, width)
    second = local_attention(grouped, own, 1, weights, wqt, wvt)
    return finish(carriers, own, weights, w_out, (first, second), grouped.shape)


def carriers_first(normed, sums, weights, w_out, groups, window):
    width = normed.shape[-1]
    own, copies = own_carriers(exchange(sums, "window", groups), sums.shape[1], window)
    near = exchange(copies, "window").reshape(-1, width)
    carriers = spread(near, "inline").reshape(-1, width)
    normed, carriers = lax.optimization_barrier((normed, carriers))
    grouped = exchange(normed, "window", groups)
    wqt, wvt = turn(weights)
    glob = glob_of(carriers, own, weights)
    return whole_attention(grouped, own, glob, weights, wqt, wvt, w_out)


def body(tokens, weights, w_out):
    window = lax.axis_size("window")
    width = tokens.shape[-1]
    groups = [[h * WIN + l for l in range(WIN)] for h in range(window // WIN)]
    rows = tokens.reshape(WIN, -1, width)
    normed, sums = normalize(rows)
    update = lax.cond(
        lax.axis_index("replica") % 2 == 0,
        lambda *args: slab_first(*args, groups, window),
        lambda *args: carriers_first(*args, groups, window),
        normed, sums, weights, w_out,
    )
    return exchange(update, "window", groups).reshape(tokens.shape)


def solution(mesh):
    return jax.shard_map(
        body,
        mesh=mesh,
        in_specs=(P(("replica", "inline", "window"), None, None, None), P(), P()),
        out_specs=P(("replica", "inline", "window"), None, None, None),
        check_vma=False,
    )
```

```python
import jax
import jax.numpy as jnp
from jax import lax
from jax.experimental import pallas as pl
from jax.experimental.pallas import tpu as pltpu
from jax.sharding import PartitionSpec as P

EMBED_SPAN = 512
HEADS = 16
HEAD_DIM = EMBED_SPAN // HEADS
WIN = 8
EPSILON = 1e-05
LOG2E = 1.4426950408889634
SCALE = HEAD_DIM ** (-0.5)
F32 = jnp.float32
BF16 = jnp.bfloat16
NT = (((1,), (1,)), ((), ()))
TN = (((0,), (0,)), ((), ()))
PARAMS = pltpu.CompilerParams(vmem_limit_bytes=32 * 1024 * 1024)


def cost(flops, size, transcendentals=0):
    return pl.CostEstimate(flops=flops, bytes_accessed=size, transcendentals=transcendentals)


def in_hbm(*arrays):
    return [pltpu.with_memory_space_constraint(a, pltpu.HBM) for a in arrays]


def standardize(values):
    center = values - jnp.mean(values, axis=-1, keepdims=True)
    spread = jnp.mean(center * center, axis=-1, keepdims=True)
    return center * lax.rsqrt(spread + EPSILON)


def norm_kernel(x_ref, normed_ref, sums_ref):
    dests, tokens, width = x_ref.shape
    cell = WIN * WIN
    normed = standardize(x_ref[...].astype(F32)).astype(BF16)
    normed_ref[...] = normed
    sums_ref[...] = jnp.sum(normed.astype(F32).reshape(dests, tokens // cell, cell, width), axis=2)


def normalize(rows):
    dests, tokens, width = rows.shape
    steps = 4
    cells = tokens // (WIN * WIN)
    block = pl.BlockSpec((dests // steps, tokens, width), lambda i: (i, 0, 0))
    return pl.pallas_call(
        norm_kernel,
        grid=(steps,),
        in_specs=[block],
        out_specs=[block, pl.BlockSpec((dests // steps, cells, width), lambda i: (i, 0, 0))],
        out_shape=[jax.ShapeDtypeStruct(rows.shape, BF16), jax.ShapeDtypeStruct((dests, cells, width), F32)],
        compiler_params=PARAMS,
        cost_estimate=cost(10_000_000, 2 << 20),
    )(*in_hbm(rows))


def turn_kernel(wq_ref, wv_ref, wqt_ref, wvt_ref):
    row = lax.broadcasted_iota(jnp.int32, (EMBED_SPAN, EMBED_SPAN), 0)
    lane = lax.broadcasted_iota(jnp.int32, (EMBED_SPAN, EMBED_SPAN), 1)
    eye = jnp.where(row == lane, 1.0, 0.0).astype(BF16)
    wqt_ref[...] = lax.dot_general(eye, wq_ref[...], NT, preferred_element_type=F32).astype(BF16)
    wvt_ref[...] = lax.dot_general(eye, wv_ref[...], NT, preferred_element_type=F32).astype(BF16)


def turn(weights):
    width = weights.shape[0]
    square = pltpu.HBM((width, width), BF16)
    whole = pl.BlockSpec((width, width), lambda i: (0, 0))
    (weights,) = in_hbm(weights)
    return pl.pallas_call(
        turn_kernel,
        grid=(1,),
        in_specs=[whole, pl.BlockSpec((width, width), lambda i: (0, 2))],
        out_specs=[whole, whole],
        out_shape=[square, square],
        compiler_params=PARAMS,
        cost_estimate=cost(600_000_000, 2 << 20),
    )(weights, weights)


def carrier_kernel(x_ref, out_ref, copies_ref):
    own_count, rows, width = out_ref.shape
    tokens = x_ref.shape[1] // own_count
    own = []
    for c in range(own_count):
        cube = x_ref[:, c * tokens : (c + 1) * tokens, :].astype(F32)
        mean = jnp.sum(jnp.sum(cube, axis=0), axis=0, keepdims=True) * (1.0 / WIN**3)
        own.append(standardize(mean))
        out_ref[c] = jnp.broadcast_to(own[-1].astype(BF16).astype(F32), (rows, width))
    copies_ref[...] = jnp.broadcast_to(jnp.concatenate(own, axis=0)[None], copies_ref.shape).astype(BF16)


def own_carriers(values, own_count, window):
    width = values.shape[-1]
    return pl.pallas_call(
        carrier_kernel,
        out_shape=[jax.ShapeDtypeStruct((own_count, 8, width), F32), jax.ShapeDtypeStruct((window, own_count, width), BF16)],
        compiler_params=PARAMS,
        cost_estimate=cost(1_000_000, 1 << 20),
    )(values)


def head_mask(rows):
    lane = lax.broadcasted_iota(jnp.int32, (rows, EMBED_SPAN), 1) // HEAD_DIM
    row = lax.broadcasted_iota(jnp.int32, (rows, EMBED_SPAN), 0) % HEADS
    return lane == row


def widen(column, count):
    return jnp.concatenate([column] * (count // 128), axis=1)


def attend(x_ref, car_ref, wk_ref, wqt_ref, wvt_ref, k_s, qh_s, ql_s, vt_s, sc_s, vc_s, write):
    count = WIN**3
    x = x_ref[...].reshape(count, EMBED_SPAN)
    k_s[...] = jnp.dot(x, wk_ref[...], preferred_element_type=F32).astype(BF16)
    q = lax.dot_general(wqt_ref[...], x, NT, preferred_element_type=F32).astype(BF16).astype(F32) * (SCALE * LOG2E)
    high = q.astype(BF16)
    low = (q - high.astype(F32)).astype(BF16)
    qh_s[...] = high
    ql_s[...] = low
    vt_s[...] = lax.dot_general(wvt_ref[...], x, NT, preferred_element_type=F32).astype(BF16)
    carrier = jnp.broadcast_to(car_ref[0, 0:1, :], (128, EMBED_SPAN)).astype(BF16)
    kc = jnp.dot(carrier[:16], wk_ref[...], preferred_element_type=F32)
    kc = jnp.where(head_mask(HEADS), kc, 0.0).astype(BF16)
    sc_s[...] = jnp.dot(kc, high, preferred_element_type=F32) + jnp.dot(kc, low, preferred_element_type=F32)
    vc_s[...] = lax.dot_general(wvt_ref[...], carrier, NT, preferred_element_type=F32).astype(BF16).astype(F32)
    ones = jnp.ones((16, count), BF16)

    def scores(h):
        group, j = h // 4, h % 4
        keys = k_s[:, group * 128 : (group + 1) * 128]
        rows = slice(h * HEAD_DIM, (h + 1) * HEAD_DIM)
        before = [jnp.zeros((HEAD_DIM * j, count), BF16)] if j else []
        after = [jnp.zeros((HEAD_DIM * (3 - j), count), BF16)] if j < 3 else []
        queries = before + [qh_s[rows, :]] + after + before + [ql_s[rows, :]] + after
        return jnp.dot(jnp.concatenate([keys, keys], axis=1), jnp.concatenate(queries, axis=0), preferred_element_type=F32)

    def mix(h, s):
        rows = slice(h * HEAD_DIM, (h + 1) * HEAD_DIM)
        sc = sc_s[h : h + 1, :]
        top = jnp.maximum(jnp.max(s, axis=0, keepdims=True), sc)
        weights = jnp.exp2(s - top).astype(BF16)
        pc = jnp.exp2(sc - top)
        values = jnp.concatenate([vt_s[rows, :], ones], axis=0)
        o = jnp.dot(values, weights, preferred_element_type=F32)
        total = o[HEAD_DIM : HEAD_DIM + 1] + pc
        write(rows, (o[:HEAD_DIM] + widen(vc_s[rows, :], count) * pc.astype(BF16).astype(F32)) / total)

    ahead = []
    for h in range(HEADS):
        ahead.append((h, scores(h)))
        if len(ahead) > 2:
            mix(*ahead.pop(0))
    for item in ahead:
        mix(*item)


def attend_scratch():
    count = WIN**3
    half = pltpu.VMEM((EMBED_SPAN, count), BF16)
    return [pltpu.VMEM((count, EMBED_SPAN), BF16), half, half, half, pltpu.VMEM((HEADS, count), F32), pltpu.VMEM((EMBED_SPAN, 128), F32)]


def whole_kernel(x_ref, car_ref, glob_ref, wk_ref, wqt_ref, wvt_ref, wo_ref, out_ref, inner_s, gl_s, *scratch):
    gl_s[...] = jnp.broadcast_to(glob_ref[0, 0:1, :], (128, EMBED_SPAN)).T

    def write(rows, local):
        inner_s[rows, :] = (local + widen(gl_s[rows, :], local.shape[1])).astype(BF16)

    attend(x_ref, car_ref, wk_ref, wqt_ref, wvt_ref, *scratch, write)
    update = lax.dot_general(inner_s[...], wo_ref[...], TN, preferred_element_type=F32)
    out_ref[...] = update.astype(BF16).reshape(out_ref.shape)


def whole_attention(grouped, own, glob, weights, wqt, wvt, w_out):
    rows, tokens, width = grouped.shape
    cell = WIN * WIN
    count = rows * cell
    cube = pl.BlockSpec((rows, cell, width), lambda i: (0, i, 0))
    row = pl.BlockSpec((1, 8, width), lambda i: (i, 0, 0))
    whole = pl.BlockSpec((width, width), lambda i: (0, 0))
    return pl.pallas_call(
        whole_kernel,
        grid=(tokens // cell,),
        in_specs=[cube, row, row, pl.BlockSpec((width, width), lambda i: (0, 1)), whole, whole, whole],
        out_specs=cube,
        out_shape=jax.ShapeDtypeStruct(grouped.shape, BF16),
        scratch_shapes=[pltpu.VMEM((width, count), BF16), pltpu.VMEM((width, 128), F32)] + attend_scratch(),
        compiler_params=PARAMS,
        cost_estimate=cost(17_000_000_000, 6 << 20, 8 << 20),
    )(grouped, own, glob, *in_hbm(weights, wqt, wvt, w_out))


def carrier_match(all_ref, w_ref):
    match = jnp.dot(all_ref[...], w_ref[:, EMBED_SPAN:], preferred_element_type=F32).astype(BF16)
    return match[:, :EMBED_SPAN], match[:, EMBED_SPAN:]


def carrier_attention(own, w_ref, keys, values):
    mask = head_mask(HEADS)
    own = jnp.broadcast_to(own, (16, EMBED_SPAN)).astype(BF16)
    queries = jnp.dot(own, w_ref[:, :EMBED_SPAN], preferred_element_type=F32)
    queries = jnp.where(mask, queries, 0.0).astype(BF16)
    s = lax.dot_general(queries, keys, NT, preferred_element_type=F32) * SCALE
    weights = jnp.exp(s - jnp.max(s, axis=-1, keepdims=True))
    total = jnp.sum(weights, axis=-1, keepdims=True)
    summed = jnp.dot(weights.astype(BF16), values, preferred_element_type=F32) / total
    return jnp.sum(jnp.where(mask, summed, 0.0), axis=0, keepdims=True)


def glob_kernel(all_ref, own_ref, w_ref, out_ref):
    keys, values = carrier_match(all_ref, w_ref)
    for c in range(out_ref.shape[0]):
        out_ref[c] = jnp.broadcast_to(carrier_attention(own_ref[c, 0:1, :], w_ref, keys, values), out_ref.shape[1:])


def glob_of(carriers, own, weights):
    return pl.pallas_call(
        glob_kernel,
        out_shape=jax.ShapeDtypeStruct(own.shape, F32),
        compiler_params=PARAMS,
        cost_estimate=cost(400_000_000, 2 << 20, 16384),
    )(carriers, own, weights)


def spread_kernel(all_ref, mine_ref, w_ref, wo_ref, out_ref):
    keys, values = carrier_match(all_ref, w_ref)
    cubes = mine_ref.shape[0]
    queries = jnp.dot(mine_ref[...], w_ref[:, :EMBED_SPAN], preferred_element_type=F32)
    queries = jnp.broadcast_to(queries[:, None, :], (cubes, HEADS, EMBED_SPAN)).reshape(cubes * HEADS, EMBED_SPAN)
    mask = head_mask(cubes * HEADS)
    queries = jnp.where(mask, queries, 0.0).astype(BF16)
    s = lax.dot_general(queries, keys, NT, preferred_element_type=F32) * SCALE
    weights = jnp.exp(s - jnp.max(s, axis=-1, keepdims=True))
    total = jnp.sum(weights, axis=-1, keepdims=True)
    summed = jnp.dot(weights.astype(BF16), values, preferred_element_type=F32) / total
    glob = jnp.sum(jnp.where(mask, summed, 0.0).reshape(cubes, HEADS, EMBED_SPAN), axis=1)
    high = glob.astype(BF16)
    low = (glob - high.astype(F32)).astype(BF16)
    out_ref[...] = jnp.dot(high, wo_ref[...], preferred_element_type=F32) + jnp.dot(low, wo_ref[...], preferred_element_type=F32)


def row_glob(carriers, mine, weights, w_out):
    return pl.pallas_call(
        spread_kernel,
        out_shape=jax.ShapeDtypeStruct(mine.shape, F32),
        compiler_params=PARAMS,
        cost_estimate=cost(800_000_000, 3 << 20, 65536),
    )(carriers, mine, weights, w_out)


def add_kernel(x_ref, g_ref, out_ref):
    rows, tokens, width = x_ref.shape
    cells = g_ref.shape[1]
    x = x_ref[...].astype(F32).reshape(rows, cells, tokens // cells, width)
    out_ref[...] = (x + g_ref[...][:, :, None, :]).astype(BF16).reshape(x_ref.shape)


def add_glob(returned, glob):
    dests, tokens, width = returned.shape
    steps = 4
    block = pl.BlockSpec((dests // steps, tokens, width), lambda i: (i, 0, 0))
    return pl.pallas_call(
        add_kernel,
        grid=(steps,),
        in_specs=[block, pl.BlockSpec((dests // steps,) + glob.shape[1:], lambda i: (i, 0, 0))],
        out_specs=block,
        out_shape=jax.ShapeDtypeStruct(returned.shape, BF16),
        compiler_params=PARAMS,
        cost_estimate=cost(1_000_000, 2 << 20),
    )(returned, glob)


def exchange(values, axis, groups=None):
    return lax.all_to_all(values, axis, split_axis=0, concat_axis=0, tiled=True, axis_index_groups=groups)


def spread(values, axis):
    return exchange(jnp.broadcast_to(values[None], (lax.axis_size(axis),) + values.shape), axis)


def slab_first(normed, sums, weights, w_out, groups, window):
    dests, cells, width = sums.shape
    grouped = exchange(normed, "window", groups)
    own, copies = own_carriers(grouped, cells, window)
    wqt, wvt = turn(weights)
    near = exchange(copies, "window").reshape(-1, width)
    update = whole_attention(grouped, own, jnp.zeros_like(own), weights, wqt, wvt, w_out)
    update, near = lax.optimization_barrier((update, near))
    returned = exchange(update, "window", groups)
    carriers = lax.all_gather(near, "inline", axis=0, tiled=True)
    cubes = dests * cells
    mine = lax.dynamic_slice_in_dim(near, lax.axis_index("window") // WIN * cubes, cubes, 0)
    return returned, row_glob(carriers, mine, weights, w_out).reshape(sums.shape)


def carriers_first(normed, sums, weights, w_out, groups, window):
    width = normed.shape[-1]
    own, copies = own_carriers(exchange(sums, "window", groups), sums.shape[1], window)
    near = exchange(copies, "window").reshape(-1, width)
    normed, near = lax.optimization_barrier((normed, near))
    grouped = exchange(normed, "window", groups)
    wqt, wvt = turn(weights)
    carriers = lax.all_gather(near, "inline", axis=0, tiled=True)
    glob = glob_of(carriers, own, weights)
    update = whole_attention(grouped, own, glob, weights, wqt, wvt, w_out)
    return exchange(update, "window", groups), jnp.zeros_like(sums)


def body(tokens, weights, w_out):
    window = lax.axis_size("window")
    width = tokens.shape[-1]
    groups = [[h * WIN + l for l in range(WIN)] for h in range(window // WIN)]
    rows = tokens.reshape(WIN, -1, width)
    normed, sums = normalize(rows)
    returned, glob = lax.cond(
        lax.axis_index("replica") % 2 == 0,
        lambda *args: slab_first(*args, groups, window),
        lambda *args: carriers_first(*args, groups, window),
        normed, sums, weights, w_out,
    )
    return add_glob(returned, glob).reshape(tokens.shape)


def solution(mesh):
    return jax.shard_map(
        body,
        mesh=mesh,
        in_specs=(P(("replica", "inline", "window"), None, None, None), P(), P()),
        out_specs=P(("replica", "inline", "window"), None, None, None),
        check_vma=False,
    )
```

```python
import jax
import jax.numpy as jnp
from jax import lax
from jax.experimental import pallas as pl
from jax.experimental.pallas import tpu as pltpu
from jax.sharding import PartitionSpec as P

EMBED_SPAN = 512
HEADS = 16
HEAD_DIM = EMBED_SPAN // HEADS
WIN = 8
EPSILON = 1e-05
LOG2E = 1.4426950408889634
SCALE = HEAD_DIM ** (-0.5)
F32 = jnp.float32
BF16 = jnp.bfloat16
NT = (((1,), (1,)), ((), ()))
TN = (((0,), (0,)), ((), ()))
PARAMS = pltpu.CompilerParams(vmem_limit_bytes=32 * 1024 * 1024)


def cost(flops, size, transcendentals=0):
    return pl.CostEstimate(flops=flops, bytes_accessed=size, transcendentals=transcendentals)


def in_hbm(*arrays):
    return [pltpu.with_memory_space_constraint(a, pltpu.HBM) for a in arrays]


def standardize(values):
    center = values - jnp.mean(values, axis=-1, keepdims=True)
    spread = jnp.mean(center * center, axis=-1, keepdims=True)
    return center * lax.rsqrt(spread + EPSILON)


def norm_kernel(x_ref, normed_ref, sums_ref):
    dests, tokens, width = x_ref.shape
    cell = WIN * WIN
    normed = standardize(x_ref[...].astype(F32)).astype(BF16)
    normed_ref[...] = normed
    sums_ref[...] = jnp.sum(normed.astype(F32).reshape(dests, tokens // cell, cell, width), axis=2)


def normalize(rows):
    dests, tokens, width = rows.shape
    steps = 2
    cells = tokens // (WIN * WIN)
    block = pl.BlockSpec((dests // steps, tokens, width), lambda i: (i, 0, 0))
    return pl.pallas_call(
        norm_kernel,
        grid=(steps,),
        in_specs=[block],
        out_specs=[block, pl.BlockSpec((dests // steps, cells, width), lambda i: (i, 0, 0))],
        out_shape=[jax.ShapeDtypeStruct(rows.shape, BF16), jax.ShapeDtypeStruct((dests, cells, width), F32)],
        compiler_params=PARAMS,
        cost_estimate=cost(10_000_000, 2 << 20),
    )(*in_hbm(rows))


def turn_kernel(wq_ref, wv_ref, wqt_ref, wvt_ref):
    row = lax.broadcasted_iota(jnp.int32, (EMBED_SPAN, EMBED_SPAN), 0)
    lane = lax.broadcasted_iota(jnp.int32, (EMBED_SPAN, EMBED_SPAN), 1)
    eye = jnp.where(row == lane, 1.0, 0.0).astype(BF16)
    wqt_ref[...] = lax.dot_general(eye, wq_ref[...], NT, preferred_element_type=F32).astype(BF16)
    wvt_ref[...] = lax.dot_general(eye, wv_ref[...], NT, preferred_element_type=F32).astype(BF16)


def turn(weights):
    width = weights.shape[0]
    square = pltpu.HBM((width, width), BF16)
    whole = pl.BlockSpec((width, width), lambda i: (0, 0))
    (weights,) = in_hbm(weights)
    return pl.pallas_call(
        turn_kernel,
        grid=(1,),
        in_specs=[whole, pl.BlockSpec((width, width), lambda i: (0, 2))],
        out_specs=[whole, whole],
        out_shape=[square, square],
        compiler_params=PARAMS,
        cost_estimate=cost(600_000_000, 2 << 20),
    )(weights, weights)


def carrier_kernel(x_ref, out_ref, copies_ref):
    own_count, rows, width = out_ref.shape
    tokens = x_ref.shape[1] // own_count
    own = []
    for c in range(own_count):
        cube = x_ref[:, c * tokens : (c + 1) * tokens, :].astype(F32)
        mean = jnp.sum(jnp.sum(cube, axis=0), axis=0, keepdims=True) * (1.0 / WIN**3)
        own.append(standardize(mean))
        out_ref[c] = jnp.broadcast_to(own[-1].astype(BF16).astype(F32), (rows, width))
    copies_ref[...] = jnp.broadcast_to(jnp.concatenate(own, axis=0)[None], copies_ref.shape).astype(BF16)


def own_carriers(values, own_count, window):
    width = values.shape[-1]
    return pl.pallas_call(
        carrier_kernel,
        out_shape=[jax.ShapeDtypeStruct((own_count, 8, width), F32), jax.ShapeDtypeStruct((window, own_count, width), BF16)],
        compiler_params=PARAMS,
        cost_estimate=cost(1_000_000, 1 << 20),
    )(values)


def head_mask(rows):
    lane = lax.broadcasted_iota(jnp.int32, (rows, EMBED_SPAN), 1) // HEAD_DIM
    row = lax.broadcasted_iota(jnp.int32, (rows, EMBED_SPAN), 0) % HEADS
    return lane == row


def widen(column, count):
    return jnp.concatenate([column] * (count // 128), axis=1)


def attend(x_ref, car_ref, wk_ref, wqt_ref, wvt_ref, k_s, qh_s, ql_s, vt_s, sc_s, vc_s, write):
    count = WIN**3
    x = x_ref[...].reshape(count, EMBED_SPAN)
    k_s[...] = jnp.dot(x, wk_ref[...], preferred_element_type=F32).astype(BF16)
    q = lax.dot_general(wqt_ref[...], x, NT, preferred_element_type=F32).astype(BF16).astype(F32) * (SCALE * LOG2E)
    high = q.astype(BF16)
    low = (q - high.astype(F32)).astype(BF16)
    qh_s[...] = high
    ql_s[...] = low
    vt_s[...] = lax.dot_general(wvt_ref[...], x, NT, preferred_element_type=F32).astype(BF16)
    carrier = jnp.broadcast_to(car_ref[0, 0:1, :], (128, EMBED_SPAN)).astype(BF16)
    kc = jnp.dot(carrier[:16], wk_ref[...], preferred_element_type=F32)
    kc = jnp.where(head_mask(HEADS), kc, 0.0).astype(BF16)
    sc_s[...] = jnp.dot(kc, high, preferred_element_type=F32) + jnp.dot(kc, low, preferred_element_type=F32)
    vc_s[...] = lax.dot_general(wvt_ref[...], carrier, NT, preferred_element_type=F32).astype(BF16).astype(F32)
    ones = jnp.ones((16, count), BF16)

    def scores(h):
        group, j = h // 4, h % 4
        keys = k_s[:, group * 128 : (group + 1) * 128]
        rows = slice(h * HEAD_DIM, (h + 1) * HEAD_DIM)
        before = [jnp.zeros((HEAD_DIM * j, count), BF16)] if j else []
        after = [jnp.zeros((HEAD_DIM * (3 - j), count), BF16)] if j < 3 else []
        queries = before + [qh_s[rows, :]] + after + before + [ql_s[rows, :]] + after
        return jnp.dot(jnp.concatenate([keys, keys], axis=1), jnp.concatenate(queries, axis=0), preferred_element_type=F32)

    def mix(h, s):
        rows = slice(h * HEAD_DIM, (h + 1) * HEAD_DIM)
        sc = sc_s[h : h + 1, :]
        top = jnp.maximum(jnp.max(s, axis=0, keepdims=True), sc)
        weights = jnp.exp2(s - top).astype(BF16)
        pc = jnp.exp2(sc - top)
        values = jnp.concatenate([vt_s[rows, :], ones], axis=0)
        o = jnp.dot(values, weights, preferred_element_type=F32)
        total = o[HEAD_DIM : HEAD_DIM + 1] + pc
        write(rows, (o[:HEAD_DIM] + widen(vc_s[rows, :], count) * pc.astype(BF16).astype(F32)) / total)

    ahead = []
    for h in range(HEADS):
        ahead.append((h, scores(h)))
        if len(ahead) > 2:
            mix(*ahead.pop(0))
    for item in ahead:
        mix(*item)


def attend_scratch():
    count = WIN**3
    half = pltpu.VMEM((EMBED_SPAN, count), BF16)
    return [pltpu.VMEM((count, EMBED_SPAN), BF16), half, half, half, pltpu.VMEM((HEADS, count), F32), pltpu.VMEM((EMBED_SPAN, 128), F32)]


def whole_kernel(x_ref, car_ref, glob_ref, wk_ref, wqt_ref, wvt_ref, wo_ref, out_ref, inner_s, gl_s, *scratch):
    gl_s[...] = jnp.broadcast_to(glob_ref[0, 0:1, :], (128, EMBED_SPAN)).T

    def write(rows, local):
        inner_s[rows, :] = (local + widen(gl_s[rows, :], local.shape[1])).astype(BF16)

    attend(x_ref, car_ref, wk_ref, wqt_ref, wvt_ref, *scratch, write)
    update = lax.dot_general(inner_s[...], wo_ref[...], TN, preferred_element_type=F32)
    out_ref[...] = update.astype(BF16).reshape(out_ref.shape)


def whole_attention(grouped, own, glob, weights, wqt, wvt, w_out):
    rows, tokens, width = grouped.shape
    cell = WIN * WIN
    count = rows * cell
    cube = pl.BlockSpec((rows, cell, width), lambda i: (0, i, 0))
    row = pl.BlockSpec((1, 8, width), lambda i: (i, 0, 0))
    whole = pl.BlockSpec((width, width), lambda i: (0, 0))
    return pl.pallas_call(
        whole_kernel,
        grid=(tokens // cell,),
        in_specs=[cube, row, row, pl.BlockSpec((width, width), lambda i: (0, 1)), whole, whole, whole],
        out_specs=cube,
        out_shape=jax.ShapeDtypeStruct(grouped.shape, BF16),
        scratch_shapes=[pltpu.VMEM((width, count), BF16), pltpu.VMEM((width, 128), F32)] + attend_scratch(),
        compiler_params=PARAMS,
        cost_estimate=cost(17_000_000_000, 6 << 20, 8 << 20),
    )(grouped, own, glob, *in_hbm(weights, wqt, wvt, w_out))


def carrier_match(all_ref, w_ref):
    match = jnp.dot(all_ref[...], w_ref[:, EMBED_SPAN:], preferred_element_type=F32).astype(BF16)
    return match[:, :EMBED_SPAN], match[:, EMBED_SPAN:]


def carrier_attention(own, w_ref, keys, values):
    mask = head_mask(HEADS)
    own = jnp.broadcast_to(own, (16, EMBED_SPAN)).astype(BF16)
    queries = jnp.dot(own, w_ref[:, :EMBED_SPAN], preferred_element_type=F32)
    queries = jnp.where(mask, queries, 0.0).astype(BF16)
    s = lax.dot_general(queries, keys, NT, preferred_element_type=F32) * SCALE
    weights = jnp.exp(s - jnp.max(s, axis=-1, keepdims=True))
    total = jnp.sum(weights, axis=-1, keepdims=True)
    summed = jnp.dot(weights.astype(BF16), values, preferred_element_type=F32) / total
    return jnp.sum(jnp.where(mask, summed, 0.0), axis=0, keepdims=True)


def glob_kernel(all_ref, own_ref, w_ref, out_ref):
    keys, values = carrier_match(all_ref, w_ref)
    for c in range(out_ref.shape[0]):
        out_ref[c] = jnp.broadcast_to(carrier_attention(own_ref[c, 0:1, :], w_ref, keys, values), out_ref.shape[1:])


def glob_of(carriers, own, weights):
    return pl.pallas_call(
        glob_kernel,
        out_shape=jax.ShapeDtypeStruct(own.shape, F32),
        compiler_params=PARAMS,
        cost_estimate=cost(400_000_000, 2 << 20, 16384),
    )(carriers, own, weights)


def spread_kernel(all_ref, mine_ref, w_ref, wo_ref, out_ref):
    keys, values = carrier_match(all_ref, w_ref)
    cubes = mine_ref.shape[0]
    queries = jnp.dot(mine_ref[...], w_ref[:, :EMBED_SPAN], preferred_element_type=F32)
    queries = jnp.broadcast_to(queries[:, None, :], (cubes, HEADS, EMBED_SPAN)).reshape(cubes * HEADS, EMBED_SPAN)
    mask = head_mask(cubes * HEADS)
    queries = jnp.where(mask, queries, 0.0).astype(BF16)
    s = lax.dot_general(queries, keys, NT, preferred_element_type=F32) * SCALE
    weights = jnp.exp(s - jnp.max(s, axis=-1, keepdims=True))
    total = jnp.sum(weights, axis=-1, keepdims=True)
    summed = jnp.dot(weights.astype(BF16), values, preferred_element_type=F32) / total
    glob = jnp.sum(jnp.where(mask, summed, 0.0).reshape(cubes, HEADS, EMBED_SPAN), axis=1)
    high = glob.astype(BF16)
    low = (glob - high.astype(F32)).astype(BF16)
    out_ref[...] = jnp.dot(high, wo_ref[...], preferred_element_type=F32) + jnp.dot(low, wo_ref[...], preferred_element_type=F32)


def row_glob(carriers, mine, weights, w_out):
    return pl.pallas_call(
        spread_kernel,
        out_shape=jax.ShapeDtypeStruct(mine.shape, F32),
        compiler_params=PARAMS,
        cost_estimate=cost(800_000_000, 3 << 20, 65536),
    )(carriers, mine, weights, w_out)


def add_kernel(x_ref, g_ref, out_ref):
    rows, tokens, width = x_ref.shape
    cells = g_ref.shape[1]
    x = x_ref[...].astype(F32).reshape(rows, cells, tokens // cells, width)
    out_ref[...] = (x + g_ref[...][:, :, None, :]).astype(BF16).reshape(x_ref.shape)


def add_glob(returned, glob):
    dests, tokens, width = returned.shape
    steps = 2
    block = pl.BlockSpec((dests // steps, tokens, width), lambda i: (i, 0, 0))
    return pl.pallas_call(
        add_kernel,
        grid=(steps,),
        in_specs=[block, pl.BlockSpec((dests // steps,) + glob.shape[1:], lambda i: (i, 0, 0))],
        out_specs=block,
        out_shape=jax.ShapeDtypeStruct(returned.shape, BF16),
        compiler_params=PARAMS,
        cost_estimate=cost(1_000_000, 2 << 20),
    )(returned, glob)


def exchange(values, axis, groups=None):
    return lax.all_to_all(values, axis, split_axis=0, concat_axis=0, tiled=True, axis_index_groups=groups)


def spread(values, axis):
    return exchange(jnp.broadcast_to(values[None], (lax.axis_size(axis),) + values.shape), axis)


def slab_first(normed, sums, weights, w_out, groups, window):
    dests, cells, width = sums.shape
    grouped = exchange(normed, "window", groups)
    own, copies = own_carriers(grouped, cells, window)
    wqt, wvt = turn(weights)
    near = exchange(copies, "window").reshape(-1, width)
    update = whole_attention(grouped, own, jnp.zeros_like(own), weights, wqt, wvt, w_out)
    update, near = lax.optimization_barrier((update, near))
    returned = exchange(update, "window", groups)
    carriers = gather_inline(near)
    cubes = dests * cells
    mine = lax.dynamic_slice_in_dim(near, lax.axis_index("window") // WIN * cubes, cubes, 0)
    return returned, row_glob(carriers, mine, weights, w_out).reshape(sums.shape)


def carriers_first(normed, sums, weights, w_out, groups, window):
    width = normed.shape[-1]
    own, copies = own_carriers(exchange(sums, "window", groups), sums.shape[1], window)
    near = exchange(copies, "window").reshape(-1, width)
    normed, near = lax.optimization_barrier((normed, near))
    grouped = exchange(normed, "window", groups)
    wqt, wvt = turn(weights)
    carriers = gather_inline(near)
    glob = glob_of(carriers, own, weights)
    update = whole_attention(grouped, own, glob, weights, wqt, wvt, w_out)
    return exchange(update, "window", groups), jnp.zeros_like(sums)


def gather_inline(rows):
    count = lax.axis_size("inline")
    step = 1
    while step < count:
        other = lax.ppermute(rows, "inline", [(i, i ^ step) for i in range(count)])
        rows = jnp.concatenate([rows, other], axis=0)
        step *= 2
    return rows


def body(tokens, weights, w_out):
    window = lax.axis_size("window")
    width = tokens.shape[-1]
    groups = [[h * WIN + l for l in range(WIN)] for h in range(window // WIN)]
    rows = tokens.reshape(WIN, -1, width)
    normed, sums = normalize(rows)
    returned, glob = lax.cond(
        lax.axis_index("replica") % 2 == 0,
        lambda *args: slab_first(*args, groups, window),
        lambda *args: carriers_first(*args, groups, window),
        normed, sums, weights, w_out,
    )
    return add_glob(returned, glob).reshape(tokens.shape)


def solution(mesh):
    return jax.shard_map(
        body,
        mesh=mesh,
        in_specs=(P(("replica", "inline", "window"), None, None, None), P(), P()),
        out_specs=P(("replica", "inline", "window"), None, None, None),
        check_vma=False,
    )
```

```python
import jax
import jax.numpy as jnp
from jax import lax
from jax.experimental import pallas as pl
from jax.experimental.pallas import tpu as pltpu
from jax.sharding import PartitionSpec as P

EMBED_SPAN = 512
HEADS = 16
HEAD_DIM = EMBED_SPAN // HEADS
WIN = 8
EPSILON = 1e-05
LOG2E = 1.4426950408889634
SCALE = HEAD_DIM ** (-0.5)
F32 = jnp.float32
BF16 = jnp.bfloat16
NT = (((1,), (1,)), ((), ()))
TN = (((0,), (0,)), ((), ()))
PARAMS = pltpu.CompilerParams(vmem_limit_bytes=32 * 1024 * 1024)


def cost(flops, size, transcendentals=0):
    return pl.CostEstimate(flops=flops, bytes_accessed=size, transcendentals=transcendentals)


def in_hbm(*arrays):
    return [pltpu.with_memory_space_constraint(a, pltpu.HBM) for a in arrays]


def standardize(values):
    center = values - jnp.mean(values, axis=-1, keepdims=True)
    spread = jnp.mean(center * center, axis=-1, keepdims=True)
    return center * lax.rsqrt(spread + EPSILON)


def norm_kernel(x_ref, normed_ref, sums_ref):
    dests, tokens, width = x_ref.shape
    cell = WIN * WIN
    normed = standardize(x_ref[...].astype(F32)).astype(BF16)
    normed_ref[...] = normed
    sums_ref[...] = jnp.sum(normed.astype(F32).reshape(dests, tokens // cell, cell, width), axis=2)


def normalize(rows):
    dests, tokens, width = rows.shape
    steps = 2
    cells = tokens // (WIN * WIN)
    block = pl.BlockSpec((dests // steps, tokens, width), lambda i: (i, 0, 0))
    return pl.pallas_call(
        norm_kernel,
        grid=(steps,),
        in_specs=[block],
        out_specs=[block, pl.BlockSpec((dests // steps, cells, width), lambda i: (i, 0, 0))],
        out_shape=[jax.ShapeDtypeStruct(rows.shape, BF16), jax.ShapeDtypeStruct((dests, cells, width), F32)],
        compiler_params=PARAMS,
        cost_estimate=cost(10_000_000, 2 << 20),
    )(*in_hbm(rows))


def turn_kernel(wq_ref, wv_ref, wqt_ref, wvt_ref):
    row = lax.broadcasted_iota(jnp.int32, (EMBED_SPAN, EMBED_SPAN), 0)
    lane = lax.broadcasted_iota(jnp.int32, (EMBED_SPAN, EMBED_SPAN), 1)
    eye = jnp.where(row == lane, 1.0, 0.0).astype(BF16)
    wqt_ref[...] = lax.dot_general(eye, wq_ref[...], NT, preferred_element_type=F32).astype(BF16)
    wvt_ref[...] = lax.dot_general(eye, wv_ref[...], NT, preferred_element_type=F32).astype(BF16)


def turn(weights):
    width = weights.shape[0]
    square = jax.ShapeDtypeStruct((width, width), BF16)
    whole = pl.BlockSpec((width, width), lambda i: (0, 0))
    (weights,) = in_hbm(weights)
    return pl.pallas_call(
        turn_kernel,
        grid=(1,),
        in_specs=[whole, pl.BlockSpec((width, width), lambda i: (0, 2))],
        out_specs=[whole, whole],
        out_shape=[square, square],
        compiler_params=PARAMS,
        cost_estimate=cost(600_000_000, 2 << 20),
    )(weights, weights)


def carrier_kernel(x_ref, out_ref, copies_ref):
    own_count, rows, width = out_ref.shape
    tokens = x_ref.shape[1] // own_count
    own = []
    for c in range(own_count):
        cube = x_ref[:, c * tokens : (c + 1) * tokens, :].astype(F32)
        mean = jnp.sum(jnp.sum(cube, axis=0), axis=0, keepdims=True) * (1.0 / WIN**3)
        own.append(standardize(mean))
        out_ref[c] = jnp.broadcast_to(own[-1].astype(BF16).astype(F32), (rows, width))
    copies_ref[...] = jnp.broadcast_to(jnp.concatenate(own, axis=0)[None], copies_ref.shape).astype(BF16)


def own_carriers(values, own_count, window):
    width = values.shape[-1]
    return pl.pallas_call(
        carrier_kernel,
        out_shape=[jax.ShapeDtypeStruct((own_count, 8, width), F32), jax.ShapeDtypeStruct((window, own_count, width), BF16)],
        compiler_params=PARAMS,
        cost_estimate=cost(1_000_000, 1 << 20),
    )(values)


def head_mask(rows):
    lane = lax.broadcasted_iota(jnp.int32, (rows, EMBED_SPAN), 1) // HEAD_DIM
    row = lax.broadcasted_iota(jnp.int32, (rows, EMBED_SPAN), 0) % HEADS
    return lane == row


def widen(column, count):
    return jnp.concatenate([column] * (count // 128), axis=1)


def attend(x_ref, car_ref, wk_ref, wqt_ref, wvt_ref, k_s, qh_s, ql_s, vt_s, sc_s, vc_s, write):
    count = WIN**3
    x = x_ref[...].reshape(count, EMBED_SPAN)
    k_s[...] = jnp.dot(x, wk_ref[...], preferred_element_type=F32).astype(BF16)
    q = lax.dot_general(wqt_ref[...], x, NT, preferred_element_type=F32).astype(BF16).astype(F32) * (SCALE * LOG2E)
    high = q.astype(BF16)
    low = (q - high.astype(F32)).astype(BF16)
    qh_s[...] = high
    ql_s[...] = low
    vt_s[...] = lax.dot_general(wvt_ref[...], x, NT, preferred_element_type=F32).astype(BF16)
    carrier = jnp.broadcast_to(car_ref[0, 0:1, :], (128, EMBED_SPAN)).astype(BF16)
    kc = jnp.dot(carrier[:16], wk_ref[...], preferred_element_type=F32)
    kc = jnp.where(head_mask(HEADS), kc, 0.0).astype(BF16)
    sc_s[...] = jnp.dot(kc, high, preferred_element_type=F32) + jnp.dot(kc, low, preferred_element_type=F32)
    vc_s[...] = lax.dot_general(wvt_ref[...], carrier, NT, preferred_element_type=F32).astype(BF16).astype(F32)
    ones = jnp.ones((16, count), BF16)

    def scores(h):
        group, j = h // 4, h % 4
        keys = k_s[:, group * 128 : (group + 1) * 128]
        rows = slice(h * HEAD_DIM, (h + 1) * HEAD_DIM)
        before = [jnp.zeros((HEAD_DIM * j, count), BF16)] if j else []
        after = [jnp.zeros((HEAD_DIM * (3 - j), count), BF16)] if j < 3 else []
        queries = before + [qh_s[rows, :]] + after + before + [ql_s[rows, :]] + after
        return jnp.dot(jnp.concatenate([keys, keys], axis=1), jnp.concatenate(queries, axis=0), preferred_element_type=F32)

    def mix(h, s):
        rows = slice(h * HEAD_DIM, (h + 1) * HEAD_DIM)
        sc = sc_s[h : h + 1, :]
        top = jnp.maximum(jnp.max(s, axis=0, keepdims=True), sc)
        weights = jnp.exp2(s - top).astype(BF16)
        pc = jnp.exp2(sc - top)
        values = jnp.concatenate([vt_s[rows, :], ones], axis=0)
        o = jnp.dot(values, weights, preferred_element_type=F32)
        total = o[HEAD_DIM : HEAD_DIM + 1] + pc
        write(rows, (o[:HEAD_DIM] + widen(vc_s[rows, :], count) * pc.astype(BF16).astype(F32)) * (1.0 / total))

    ahead = []
    for h in range(HEADS):
        ahead.append((h, scores(h)))
        if len(ahead) > 2:
            mix(*ahead.pop(0))
    for item in ahead:
        mix(*item)


def attend_scratch():
    count = WIN**3
    half = pltpu.VMEM((EMBED_SPAN, count), BF16)
    return [pltpu.VMEM((count, EMBED_SPAN), BF16), half, half, half, pltpu.VMEM((HEADS, count), F32), pltpu.VMEM((EMBED_SPAN, 128), F32)]


def whole_kernel(x_ref, car_ref, glob_ref, wk_ref, wqt_ref, wvt_ref, wo_ref, out_ref, inner_s, gl_s, *scratch):
    gl_s[...] = jnp.broadcast_to(glob_ref[0, 0:1, :], (128, EMBED_SPAN)).T

    def write(rows, local):
        inner_s[rows, :] = (local + widen(gl_s[rows, :], local.shape[1])).astype(BF16)

    attend(x_ref, car_ref, wk_ref, wqt_ref, wvt_ref, *scratch, write)
    update = lax.dot_general(inner_s[...], wo_ref[...], TN, preferred_element_type=F32)
    out_ref[...] = update.astype(BF16).reshape(out_ref.shape)


def whole_attention(grouped, own, glob, weights, wqt, wvt, w_out):
    rows, tokens, width = grouped.shape
    cell = WIN * WIN
    count = rows * cell
    cube = pl.BlockSpec((rows, cell, width), lambda i: (0, i, 0))
    row = pl.BlockSpec((1, 8, width), lambda i: (i, 0, 0))
    whole = pl.BlockSpec((width, width), lambda i: (0, 0))
    return pl.pallas_call(
        whole_kernel,
        grid=(tokens // cell,),
        in_specs=[cube, row, row, pl.BlockSpec((width, width), lambda i: (0, 1)), whole, whole, whole],
        out_specs=cube,
        out_shape=jax.ShapeDtypeStruct(grouped.shape, BF16),
        scratch_shapes=[pltpu.VMEM((width, count), BF16), pltpu.VMEM((width, 128), F32)] + attend_scratch(),
        compiler_params=PARAMS,
        cost_estimate=cost(17_000_000_000, 6 << 20, 8 << 20),
    )(grouped, own, glob, weights, wqt, wvt, w_out)


def carrier_match(all_ref, w_ref):
    match = jnp.dot(all_ref[...], w_ref[:, EMBED_SPAN:], preferred_element_type=F32).astype(BF16)
    return match[:, :EMBED_SPAN], match[:, EMBED_SPAN:]


def carrier_attention(own, w_ref, keys, values):
    mask = head_mask(HEADS)
    own = jnp.broadcast_to(own, (16, EMBED_SPAN)).astype(BF16)
    queries = jnp.dot(own, w_ref[:, :EMBED_SPAN], preferred_element_type=F32)
    queries = jnp.where(mask, queries, 0.0).astype(BF16)
    s = lax.dot_general(queries, keys, NT, preferred_element_type=F32) * SCALE
    weights = jnp.exp(s - jnp.max(s, axis=-1, keepdims=True))
    total = jnp.sum(weights, axis=-1, keepdims=True)
    summed = jnp.dot(weights.astype(BF16), values, preferred_element_type=F32) / total
    return jnp.sum(jnp.where(mask, summed, 0.0), axis=0, keepdims=True)


def glob_kernel(all_ref, own_ref, w_ref, out_ref):
    keys, values = carrier_match(all_ref, w_ref)
    for c in range(out_ref.shape[0]):
        out_ref[c] = jnp.broadcast_to(carrier_attention(own_ref[c, 0:1, :], w_ref, keys, values), out_ref.shape[1:])


def glob_of(carriers, own, weights):
    return pl.pallas_call(
        glob_kernel,
        out_shape=jax.ShapeDtypeStruct(own.shape, F32),
        compiler_params=PARAMS,
        cost_estimate=cost(400_000_000, 2 << 20, 16384),
    )(carriers, own, weights)


def spread_kernel(all_ref, mine_ref, w_ref, wo_ref, out_ref):
    keys, values = carrier_match(all_ref, w_ref)
    cubes = mine_ref.shape[0]
    queries = jnp.dot(mine_ref[...], w_ref[:, :EMBED_SPAN], preferred_element_type=F32)
    queries = jnp.broadcast_to(queries[:, None, :], (cubes, HEADS, EMBED_SPAN)).reshape(cubes * HEADS, EMBED_SPAN)
    mask = head_mask(cubes * HEADS)
    queries = jnp.where(mask, queries, 0.0).astype(BF16)
    s = lax.dot_general(queries, keys, NT, preferred_element_type=F32) * SCALE
    weights = jnp.exp(s - jnp.max(s, axis=-1, keepdims=True))
    total = jnp.sum(weights, axis=-1, keepdims=True)
    summed = jnp.dot(weights.astype(BF16), values, preferred_element_type=F32) / total
    glob = jnp.sum(jnp.where(mask, summed, 0.0).reshape(cubes, HEADS, EMBED_SPAN), axis=1)
    high = glob.astype(BF16)
    low = (glob - high.astype(F32)).astype(BF16)
    out_ref[...] = jnp.dot(high, wo_ref[...], preferred_element_type=F32) + jnp.dot(low, wo_ref[...], preferred_element_type=F32)


def row_glob(carriers, mine, weights, w_out):
    return pl.pallas_call(
        spread_kernel,
        out_shape=jax.ShapeDtypeStruct(mine.shape, F32),
        compiler_params=PARAMS,
        cost_estimate=cost(800_000_000, 3 << 20, 65536),
    )(carriers, mine, weights, w_out)


def add_kernel(x_ref, g_ref, out_ref):
    rows, tokens, width = x_ref.shape
    cells = g_ref.shape[1]
    x = x_ref[...].astype(F32).reshape(rows, cells, tokens // cells, width)
    out_ref[...] = (x + g_ref[...][:, :, None, :]).astype(BF16).reshape(x_ref.shape)


def add_glob(returned, glob):
    dests, tokens, width = returned.shape
    steps = 2
    block = pl.BlockSpec((dests // steps, tokens, width), lambda i: (i, 0, 0))
    return pl.pallas_call(
        add_kernel,
        grid=(steps,),
        in_specs=[block, pl.BlockSpec((dests // steps,) + glob.shape[1:], lambda i: (i, 0, 0))],
        out_specs=block,
        out_shape=jax.ShapeDtypeStruct(returned.shape, BF16),
        compiler_params=PARAMS,
        cost_estimate=cost(1_000_000, 2 << 20),
    )(returned, glob)


def exchange(values, axis, groups=None):
    return lax.all_to_all(values, axis, split_axis=0, concat_axis=0, tiled=True, axis_index_groups=groups)


def spread(values, axis):
    return exchange(jnp.broadcast_to(values[None], (lax.axis_size(axis),) + values.shape), axis)


def slab_first(normed, sums, weights, w_out, groups, window):
    dests, cells, width = sums.shape
    grouped = exchange(normed, "window", groups)
    own, copies = own_carriers(grouped, cells, window)
    wqt, wvt = turn(weights)
    near = exchange(copies, "window").reshape(-1, width)
    update = whole_attention(grouped, own, jnp.zeros_like(own), weights, wqt, wvt, w_out)
    update, near = lax.optimization_barrier((update, near))
    returned = exchange(update, "window", groups)
    carriers = gather_inline(near)
    cubes = dests * cells
    mine = lax.dynamic_slice_in_dim(near, lax.axis_index("window") // WIN * cubes, cubes, 0)
    return returned, row_glob(carriers, mine, weights, w_out).reshape(sums.shape)


def carriers_first(normed, sums, weights, w_out, groups, window):
    width = normed.shape[-1]
    own, copies = own_carriers(exchange(sums, "window", groups), sums.shape[1], window)
    near = exchange(copies, "window").reshape(-1, width)
    normed, near = lax.optimization_barrier((normed, near))
    grouped = exchange(normed, "window", groups)
    wqt, wvt = turn(weights)
    carriers = gather_inline(near)
    glob = glob_of(carriers, own, weights)
    update = whole_attention(grouped, own, glob, weights, wqt, wvt, w_out)
    return exchange(update, "window", groups), jnp.zeros_like(sums)


def gather_inline(rows):
    count = lax.axis_size("inline")
    step = 1
    while step < count:
        other = lax.ppermute(rows, "inline", [(i, i ^ step) for i in range(count)])
        rows = jnp.concatenate([rows, other], axis=0)
        step *= 2
    return rows


def body(tokens, weights, w_out):
    window = lax.axis_size("window")
    width = tokens.shape[-1]
    groups = [[h * WIN + l for l in range(WIN)] for h in range(window // WIN)]
    rows = tokens.reshape(WIN, -1, width)
    normed, sums = normalize(rows)
    returned, glob = lax.cond(
        lax.axis_index("replica") % 2 == 0,
        lambda *args: slab_first(*args, groups, window),
        lambda *args: carriers_first(*args, groups, window),
        normed, sums, weights, w_out,
    )
    return add_glob(returned, glob).reshape(tokens.shape)


def solution(mesh):
    return jax.shard_map(
        body,
        mesh=mesh,
        in_specs=(P(("replica", "inline", "window"), None, None, None), P(), P()),
        out_specs=P(("replica", "inline", "window"), None, None, None),
        check_vma=False,
    )
```

```python
import jax
import jax.numpy as jnp
from jax import lax
from jax.experimental import pallas as pl
from jax.experimental.pallas import tpu as pltpu
from jax.sharding import PartitionSpec as P

EMBED_SPAN = 512
HEADS = 16
HEAD_DIM = EMBED_SPAN // HEADS
WIN = 8
EPSILON = 1e-05
LOG2E = 1.4426950408889634
SCALE = HEAD_DIM ** (-0.5)
F32 = jnp.float32
BF16 = jnp.bfloat16
NT = (((1,), (1,)), ((), ()))
TN = (((0,), (0,)), ((), ()))
PARAMS = pltpu.CompilerParams(vmem_limit_bytes=32 * 1024 * 1024)


def cost(flops, size, transcendentals=0):
    return pl.CostEstimate(flops=flops, bytes_accessed=size, transcendentals=transcendentals)


def in_hbm(*arrays):
    return [pltpu.with_memory_space_constraint(a, pltpu.HBM) for a in arrays]


def standardize(values):
    center = values - jnp.mean(values, axis=-1, keepdims=True)
    spread = jnp.mean(center * center, axis=-1, keepdims=True)
    return center * lax.rsqrt(spread + EPSILON)


def norm_kernel(x_ref, normed_ref, sums_ref):
    dests, tokens, width = x_ref.shape
    cell = WIN * WIN
    normed = standardize(x_ref[...].astype(F32)).astype(BF16)
    normed_ref[...] = normed
    sums_ref[...] = jnp.sum(normed.astype(F32).reshape(dests, tokens // cell, cell, width), axis=2)


def normalize(rows):
    dests, tokens, width = rows.shape
    steps = 2
    cells = tokens // (WIN * WIN)
    block = pl.BlockSpec((dests // steps, tokens, width), lambda i: (i, 0, 0))
    return pl.pallas_call(
        norm_kernel,
        grid=(steps,),
        in_specs=[block],
        out_specs=[block, pl.BlockSpec((dests // steps, cells, width), lambda i: (i, 0, 0))],
        out_shape=[jax.ShapeDtypeStruct(rows.shape, BF16), jax.ShapeDtypeStruct((dests, cells, width), F32)],
        compiler_params=PARAMS,
        cost_estimate=cost(10_000_000, 2 << 20),
    )(*in_hbm(rows))


def turn_kernel(wq_ref, wv_ref, wqt_ref, wvt_ref):
    row = lax.broadcasted_iota(jnp.int32, (EMBED_SPAN, EMBED_SPAN), 0)
    lane = lax.broadcasted_iota(jnp.int32, (EMBED_SPAN, EMBED_SPAN), 1)
    eye = jnp.where(row == lane, 1.0, 0.0).astype(BF16)
    wqt_ref[...] = lax.dot_general(eye, wq_ref[...], NT, preferred_element_type=F32).astype(BF16)
    wvt_ref[...] = lax.dot_general(eye, wv_ref[...], NT, preferred_element_type=F32).astype(BF16)


def turn(weights):
    width = weights.shape[0]
    square = jax.ShapeDtypeStruct((width, width), BF16)
    whole = pl.BlockSpec((width, width), lambda i: (0, 0))
    (weights,) = in_hbm(weights)
    return pl.pallas_call(
        turn_kernel,
        grid=(1,),
        in_specs=[whole, pl.BlockSpec((width, width), lambda i: (0, 2))],
        out_specs=[whole, whole],
        out_shape=[square, square],
        compiler_params=PARAMS,
        cost_estimate=cost(600_000_000, 2 << 20),
    )(weights, weights)


def carrier_kernel(x_ref, out_ref, copies_ref):
    own_count, rows, width = out_ref.shape
    tokens = x_ref.shape[1] // own_count
    own = []
    for c in range(own_count):
        cube = x_ref[:, c * tokens : (c + 1) * tokens, :].astype(F32)
        mean = jnp.sum(jnp.sum(cube, axis=0), axis=0, keepdims=True) * (1.0 / WIN**3)
        own.append(standardize(mean))
        out_ref[c] = jnp.broadcast_to(own[-1].astype(BF16).astype(F32), (rows, width))
    copies_ref[...] = jnp.broadcast_to(jnp.concatenate(own, axis=0)[None], copies_ref.shape).astype(BF16)


def own_carriers(values, own_count, window):
    width = values.shape[-1]
    return pl.pallas_call(
        carrier_kernel,
        out_shape=[jax.ShapeDtypeStruct((own_count, 8, width), F32), jax.ShapeDtypeStruct((window, own_count, width), BF16)],
        compiler_params=PARAMS,
        cost_estimate=cost(1_000_000, 1 << 20),
    )(values)


def head_mask(rows):
    lane = lax.broadcasted_iota(jnp.int32, (rows, EMBED_SPAN), 1) // HEAD_DIM
    row = lax.broadcasted_iota(jnp.int32, (rows, EMBED_SPAN), 0) % HEADS
    return lane == row


def widen(column, count):
    return jnp.concatenate([column] * (count // 128), axis=1)


def attend(x_ref, car_ref, wk_ref, wqt_ref, wvt_ref, k_s, qh_s, ql_s, vt_s, sc_s, vc_s, write):
    count = WIN**3
    x = x_ref[...].reshape(count, EMBED_SPAN)
    k_s[...] = jnp.dot(x, wk_ref[...], preferred_element_type=F32).astype(BF16)
    q = lax.dot_general(wqt_ref[...], x, NT, preferred_element_type=F32).astype(BF16).astype(F32) * (SCALE * LOG2E)
    high = q.astype(BF16)
    low = (q - high.astype(F32)).astype(BF16)
    qh_s[...] = high
    ql_s[...] = low
    vt_s[...] = lax.dot_general(wvt_ref[...], x, NT, preferred_element_type=F32).astype(BF16)
    carrier = jnp.broadcast_to(car_ref[0, 0:1, :], (128, EMBED_SPAN)).astype(BF16)
    kc = jnp.dot(carrier[:16], wk_ref[...], preferred_element_type=F32)
    kc = jnp.where(head_mask(HEADS), kc, 0.0).astype(BF16)
    sc_s[...] = jnp.dot(kc, high, preferred_element_type=F32) + jnp.dot(kc, low, preferred_element_type=F32)
    vc_s[...] = lax.dot_general(wvt_ref[...], carrier, NT, preferred_element_type=F32).astype(BF16).astype(F32)
    ones = jnp.ones((16, count), BF16)

    def scores(h):
        group, j = h // 4, h % 4
        keys = k_s[:, group * 128 : (group + 1) * 128]
        rows = slice(h * HEAD_DIM, (h + 1) * HEAD_DIM)
        before = [jnp.zeros((HEAD_DIM * j, count), BF16)] if j else []
        after = [jnp.zeros((HEAD_DIM * (3 - j), count), BF16)] if j < 3 else []
        queries = before + [qh_s[rows, :]] + after + before + [ql_s[rows, :]] + after
        return jnp.dot(jnp.concatenate([keys, keys], axis=1), jnp.concatenate(queries, axis=0), preferred_element_type=F32)

    def mix(h, s):
        rows = slice(h * HEAD_DIM, (h + 1) * HEAD_DIM)
        sc = sc_s[h : h + 1, :]
        top = jnp.maximum(jnp.max(s, axis=0, keepdims=True), sc)
        weights = jnp.exp2(s - top).astype(BF16)
        pc = jnp.exp2(sc - top)
        values = jnp.concatenate([vt_s[rows, :], ones], axis=0)
        o = jnp.dot(values, weights, preferred_element_type=F32)
        total = o[HEAD_DIM : HEAD_DIM + 1] + pc
        write(rows, (o[:HEAD_DIM] + widen(vc_s[rows, :], count) * pc.astype(BF16).astype(F32)) * (1.0 / total))

    ahead = []
    for h in range(HEADS):
        ahead.append((h, scores(h)))
        if len(ahead) > 2:
            mix(*ahead.pop(0))
    for item in ahead:
        mix(*item)


def attend_scratch():
    count = WIN**3
    half = pltpu.VMEM((EMBED_SPAN, count), BF16)
    return [pltpu.VMEM((count, EMBED_SPAN), BF16), half, half, half, pltpu.VMEM((HEADS, count), F32), pltpu.VMEM((EMBED_SPAN, 128), F32)]


def whole_kernel(x_ref, car_ref, glob_ref, wk_ref, wqt_ref, wvt_ref, wo_ref, out_ref, inner_s, gl_s, *scratch):
    gl_s[...] = jnp.broadcast_to(glob_ref[0, 0:1, :], (128, EMBED_SPAN)).T

    def write(rows, local):
        inner_s[rows, :] = (local + widen(gl_s[rows, :], local.shape[1])).astype(BF16)

    attend(x_ref, car_ref, wk_ref, wqt_ref, wvt_ref, *scratch, write)
    update = lax.dot_general(inner_s[...], wo_ref[...], TN, preferred_element_type=F32)
    out_ref[...] = update.astype(BF16).reshape(out_ref.shape)


def whole_attention(grouped, own, glob, weights, wqt, wvt, w_out):
    rows, tokens, width = grouped.shape
    cell = WIN * WIN
    count = rows * cell
    cube = pl.BlockSpec((rows, cell, width), lambda i: (0, i, 0))
    row = pl.BlockSpec((1, 8, width), lambda i: (i, 0, 0))
    whole = pl.BlockSpec((width, width), lambda i: (0, 0))
    return pl.pallas_call(
        whole_kernel,
        grid=(tokens // cell,),
        in_specs=[cube, row, row, pl.BlockSpec((width, width), lambda i: (0, 1)), whole, whole, whole],
        out_specs=cube,
        out_shape=jax.ShapeDtypeStruct(grouped.shape, BF16),
        scratch_shapes=[pltpu.VMEM((width, count), BF16), pltpu.VMEM((width, 128), F32)] + attend_scratch(),
        compiler_params=PARAMS,
        cost_estimate=cost(17_000_000_000, 6 << 20, 8 << 20),
    )(grouped, own, glob, weights, wqt, wvt, w_out)


def carrier_match(all_ref, w_ref):
    match = jnp.dot(all_ref[...], w_ref[:, EMBED_SPAN:], preferred_element_type=F32).astype(BF16)
    return match[:, :EMBED_SPAN], match[:, EMBED_SPAN:]


def carrier_attention(own, w_ref, keys, values):
    mask = head_mask(HEADS)
    own = jnp.broadcast_to(own, (16, EMBED_SPAN)).astype(BF16)
    queries = jnp.dot(own, w_ref[:, :EMBED_SPAN], preferred_element_type=F32)
    queries = jnp.where(mask, queries, 0.0).astype(BF16)
    s = lax.dot_general(queries, keys, NT, preferred_element_type=F32) * SCALE
    weights = jnp.exp(s - jnp.max(s, axis=-1, keepdims=True))
    total = jnp.sum(weights, axis=-1, keepdims=True)
    summed = jnp.dot(weights.astype(BF16), values, preferred_element_type=F32) / total
    return jnp.sum(jnp.where(mask, summed, 0.0), axis=0, keepdims=True)


def glob_kernel(all_ref, own_ref, w_ref, out_ref):
    keys, values = carrier_match(all_ref, w_ref)
    for c in range(out_ref.shape[0]):
        out_ref[c] = jnp.broadcast_to(carrier_attention(own_ref[c, 0:1, :], w_ref, keys, values), out_ref.shape[1:])


def glob_of(carriers, own, weights):
    return pl.pallas_call(
        glob_kernel,
        out_shape=jax.ShapeDtypeStruct(own.shape, F32),
        compiler_params=PARAMS,
        cost_estimate=cost(400_000_000, 2 << 20, 16384),
    )(carriers, own, weights)


def spread_kernel(all_ref, mine_ref, w_ref, wo_ref, out_ref):
    keys, values = carrier_match(all_ref, w_ref)
    cubes = mine_ref.shape[0]
    queries = jnp.dot(mine_ref[...], w_ref[:, :EMBED_SPAN], preferred_element_type=F32)
    queries = jnp.broadcast_to(queries[:, None, :], (cubes, HEADS, EMBED_SPAN)).reshape(cubes * HEADS, EMBED_SPAN)
    mask = head_mask(cubes * HEADS)
    queries = jnp.where(mask, queries, 0.0).astype(BF16)
    s = lax.dot_general(queries, keys, NT, preferred_element_type=F32) * SCALE
    weights = jnp.exp(s - jnp.max(s, axis=-1, keepdims=True))
    total = jnp.sum(weights, axis=-1, keepdims=True)
    summed = jnp.dot(weights.astype(BF16), values, preferred_element_type=F32) / total
    glob = jnp.sum(jnp.where(mask, summed, 0.0).reshape(cubes, HEADS, EMBED_SPAN), axis=1)
    high = glob.astype(BF16)
    low = (glob - high.astype(F32)).astype(BF16)
    out_ref[...] = jnp.dot(high, wo_ref[...], preferred_element_type=F32) + jnp.dot(low, wo_ref[...], preferred_element_type=F32)


def row_glob(carriers, mine, weights, w_out):
    return pl.pallas_call(
        spread_kernel,
        out_shape=jax.ShapeDtypeStruct(mine.shape, F32),
        compiler_params=PARAMS,
        cost_estimate=cost(800_000_000, 3 << 20, 65536),
    )(carriers, mine, weights, w_out)


def add_kernel(x_ref, g_ref, out_ref):
    rows, tokens, width = x_ref.shape
    cells = g_ref.shape[1]
    x = x_ref[...].astype(F32).reshape(rows, cells, tokens // cells, width)
    out_ref[...] = (x + g_ref[...][:, :, None, :]).astype(BF16).reshape(x_ref.shape)


def add_glob(returned, glob):
    dests, tokens, width = returned.shape
    steps = 2
    block = pl.BlockSpec((dests // steps, tokens, width), lambda i: (i, 0, 0))
    return pl.pallas_call(
        add_kernel,
        grid=(steps,),
        in_specs=[block, pl.BlockSpec((dests // steps,) + glob.shape[1:], lambda i: (i, 0, 0))],
        out_specs=block,
        out_shape=jax.ShapeDtypeStruct(returned.shape, BF16),
        compiler_params=PARAMS,
        cost_estimate=cost(1_000_000, 2 << 20),
    )(returned, glob)


def exchange(values, axis, groups=None):
    return lax.all_to_all(values, axis, split_axis=0, concat_axis=0, tiled=True, axis_index_groups=groups)


def spread(values, axis):
    return exchange(jnp.broadcast_to(values[None], (lax.axis_size(axis),) + values.shape), axis)


def slab_first(normed, sums, weights, w_out, groups, window):
    dests, cells, width = sums.shape
    grouped = exchange(normed, "window", groups)
    own, copies = own_carriers(grouped, cells, window)
    wqt, wvt = turn(weights)
    near = exchange(copies, "window").reshape(-1, width)
    update = whole_attention(grouped, own, jnp.zeros_like(own), weights, wqt, wvt, w_out)
    update, near = lax.optimization_barrier((update, near))
    returned = exchange(update, "window", groups)
    carriers = gather_inline(near)
    cubes = dests * cells
    mine = lax.dynamic_slice_in_dim(near, lax.axis_index("window") // WIN * cubes, cubes, 0)
    return returned, row_glob(carriers, mine, weights, w_out).reshape(sums.shape)


def carriers_first(normed, sums, weights, w_out, groups, window):
    dests, cells, width = sums.shape
    own, copies = own_carriers(exchange(sums, "window", groups), cells, window)
    normed, copies = lax.optimization_barrier((normed, copies))
    grouped = exchange(normed, "window", groups)
    wqt, wvt = turn(weights)
    grouped, copies = lax.optimization_barrier((grouped, copies))
    near = exchange(copies, "window").reshape(-1, width)
    update = whole_attention(grouped, own, jnp.zeros_like(own), weights, wqt, wvt, w_out)
    update, near = lax.optimization_barrier((update, near))
    returned = exchange(update, "window", groups)
    carriers = gather_inline(near)
    cubes = dests * cells
    mine = lax.dynamic_slice_in_dim(near, lax.axis_index("window") // WIN * cubes, cubes, 0)
    return returned, row_glob(carriers, mine, weights, w_out).reshape(sums.shape)


def gather_inline(rows):
    count = lax.axis_size("inline")
    step = 1
    while step < count:
        other = lax.ppermute(rows, "inline", [(i, i ^ step) for i in range(count)])
        rows = jnp.concatenate([rows, other], axis=0)
        step *= 2
    return rows


def body(tokens, weights, w_out):
    window = lax.axis_size("window")
    width = tokens.shape[-1]
    groups = [[h * WIN + l for l in range(WIN)] for h in range(window // WIN)]
    rows = tokens.reshape(WIN, -1, width)
    normed, sums = normalize(rows)
    returned, glob = lax.cond(
        lax.axis_index("replica") % 2 == 0,
        lambda *args: slab_first(*args, groups, window),
        lambda *args: carriers_first(*args, groups, window),
        normed, sums, weights, w_out,
    )
    return add_glob(returned, glob).reshape(tokens.shape)


def solution(mesh):
    return jax.shard_map(
        body,
        mesh=mesh,
        in_specs=(P(("replica", "inline", "window"), None, None, None), P(), P()),
        out_specs=P(("replica", "inline", "window"), None, None, None),
        check_vma=False,
    )
```

```python
import jax
import jax.numpy as jnp
from jax import lax
from jax.experimental import pallas as pl
from jax.experimental.pallas import tpu as pltpu
from jax.sharding import PartitionSpec as P

EMBED_SPAN = 512
HEADS = 16
HEAD_DIM = EMBED_SPAN // HEADS
WIN = 8
EPSILON = 1e-05
LOG2E = 1.4426950408889634
SCALE = HEAD_DIM ** (-0.5)
F32 = jnp.float32
BF16 = jnp.bfloat16
NT = (((1,), (1,)), ((), ()))
TN = (((0,), (0,)), ((), ()))
PARAMS = pltpu.CompilerParams(vmem_limit_bytes=32 * 1024 * 1024)


def cost(flops, size, transcendentals=0):
    return pl.CostEstimate(flops=flops, bytes_accessed=size, transcendentals=transcendentals)


def in_hbm(*arrays):
    return [pltpu.with_memory_space_constraint(a, pltpu.HBM) for a in arrays]


def standardize(values):
    center = values - jnp.mean(values, axis=-1, keepdims=True)
    spread = jnp.mean(center * center, axis=-1, keepdims=True)
    return center * lax.rsqrt(spread + EPSILON)


def plain_norm_kernel(x_ref, normed_ref):
    normed_ref[...] = standardize(x_ref[...].astype(F32)).astype(BF16)


def norm_kernel(x_ref, normed_ref, sums_ref):
    dests, tokens, width = x_ref.shape
    cell = WIN * WIN
    normed = standardize(x_ref[...].astype(F32)).astype(BF16)
    normed_ref[...] = normed
    sums_ref[...] = jnp.sum(normed.astype(F32).reshape(dests, tokens // cell, cell, width), axis=2)


def normalize(rows, with_sums):
    dests, tokens, width = rows.shape
    steps = 2
    cells = tokens // (WIN * WIN)
    block = pl.BlockSpec((dests // steps, tokens, width), lambda i: (i, 0, 0))
    sums_block = pl.BlockSpec((dests // steps, cells, width), lambda i: (i, 0, 0))
    sums_shape = jax.ShapeDtypeStruct((dests, cells, width), F32)
    return pl.pallas_call(
        norm_kernel if with_sums else plain_norm_kernel,
        grid=(steps,),
        in_specs=[block],
        out_specs=[block, sums_block] if with_sums else [block],
        out_shape=[jax.ShapeDtypeStruct(rows.shape, BF16)] + ([sums_shape] if with_sums else []),
        compiler_params=PARAMS,
        cost_estimate=cost(10_000_000, 2 << 20),
    )(*in_hbm(rows))


def turn_kernel(wq_ref, wv_ref, wqt_ref, wvt_ref):
    row = lax.broadcasted_iota(jnp.int32, (EMBED_SPAN, EMBED_SPAN), 0)
    lane = lax.broadcasted_iota(jnp.int32, (EMBED_SPAN, EMBED_SPAN), 1)
    eye = jnp.where(row == lane, 1.0, 0.0).astype(BF16)
    wqt_ref[...] = lax.dot_general(eye, wq_ref[...], NT, preferred_element_type=F32).astype(BF16)
    wvt_ref[...] = lax.dot_general(eye, wv_ref[...], NT, preferred_element_type=F32).astype(BF16)


def turn(weights):
    width = weights.shape[0]
    square = jax.ShapeDtypeStruct((width, width), BF16)
    whole = pl.BlockSpec((width, width), lambda i: (0, 0))
    (weights,) = in_hbm(weights)
    return pl.pallas_call(
        turn_kernel,
        grid=(1,),
        in_specs=[whole, pl.BlockSpec((width, width), lambda i: (0, 2))],
        out_specs=[whole, whole],
        out_shape=[square, square],
        compiler_params=PARAMS,
        cost_estimate=cost(600_000_000, 2 << 20),
    )(weights, weights)


def carrier_kernel(x_ref, out_ref, copies_ref):
    own_count, rows, width = out_ref.shape
    tokens = x_ref.shape[1] // own_count
    own = []
    for c in range(own_count):
        cube = x_ref[:, c * tokens : (c + 1) * tokens, :].astype(F32)
        mean = jnp.sum(jnp.sum(cube, axis=0), axis=0, keepdims=True) * (1.0 / WIN**3)
        own.append(standardize(mean))
        out_ref[c] = jnp.broadcast_to(own[-1].astype(BF16).astype(F32), (rows, width))
    copies_ref[...] = jnp.broadcast_to(jnp.concatenate(own, axis=0)[None], copies_ref.shape).astype(BF16)


def own_carriers(values, own_count, window):
    width = values.shape[-1]
    return pl.pallas_call(
        carrier_kernel,
        out_shape=[jax.ShapeDtypeStruct((own_count, 8, width), F32), jax.ShapeDtypeStruct((window, own_count, width), BF16)],
        compiler_params=PARAMS,
        cost_estimate=cost(1_000_000, 1 << 20),
    )(values)


def head_mask(rows):
    lane = lax.broadcasted_iota(jnp.int32, (rows, EMBED_SPAN), 1) // HEAD_DIM
    row = lax.broadcasted_iota(jnp.int32, (rows, EMBED_SPAN), 0) % HEADS
    return lane == row


def widen(column, count):
    return jnp.concatenate([column] * (count // 128), axis=1)


def attend(x_ref, car_ref, wk_ref, wqt_ref, wvt_ref, k_s, qh_s, ql_s, vt_s, sc_s, vc_s, write):
    count = WIN**3
    x = x_ref[...].reshape(count, EMBED_SPAN)
    k_s[...] = jnp.dot(x, wk_ref[...], preferred_element_type=F32).astype(BF16)
    q = lax.dot_general(wqt_ref[...], x, NT, preferred_element_type=F32).astype(BF16).astype(F32) * (SCALE * LOG2E)
    high = q.astype(BF16)
    low = (q - high.astype(F32)).astype(BF16)
    qh_s[...] = high
    ql_s[...] = low
    vt_s[...] = lax.dot_general(wvt_ref[...], x, NT, preferred_element_type=F32).astype(BF16)
    carrier = jnp.broadcast_to(car_ref[0, 0:1, :], (128, EMBED_SPAN)).astype(BF16)
    kc = jnp.dot(carrier[:16], wk_ref[...], preferred_element_type=F32)
    kc = jnp.where(head_mask(HEADS), kc, 0.0).astype(BF16)
    sc_s[...] = jnp.dot(kc, high, preferred_element_type=F32) + jnp.dot(kc, low, preferred_element_type=F32)
    vc_s[...] = lax.dot_general(wvt_ref[...], carrier, NT, preferred_element_type=F32).astype(BF16).astype(F32)
    ones = jnp.ones((16, count), BF16)

    def scores(h):
        group, j = h // 4, h % 4
        keys = k_s[:, group * 128 : (group + 1) * 128]
        rows = slice(h * HEAD_DIM, (h + 1) * HEAD_DIM)
        before = [jnp.zeros((HEAD_DIM * j, count), BF16)] if j else []
        after = [jnp.zeros((HEAD_DIM * (3 - j), count), BF16)] if j < 3 else []
        queries = before + [qh_s[rows, :]] + after + before + [ql_s[rows, :]] + after
        return jnp.dot(jnp.concatenate([keys, keys], axis=1), jnp.concatenate(queries, axis=0), preferred_element_type=F32)

    def mix(h, s):
        rows = slice(h * HEAD_DIM, (h + 1) * HEAD_DIM)
        sc = sc_s[h : h + 1, :]
        top = jnp.maximum(jnp.max(s, axis=0, keepdims=True), sc)
        weights = jnp.exp2(s - top).astype(BF16)
        pc = jnp.exp2(sc - top)
        values = jnp.concatenate([vt_s[rows, :], ones], axis=0)
        o = jnp.dot(values, weights, preferred_element_type=F32)
        total = o[HEAD_DIM : HEAD_DIM + 1] + pc
        write(rows, (o[:HEAD_DIM] + widen(vc_s[rows, :], count) * pc.astype(BF16).astype(F32)) * (1.0 / total))

    ahead = []
    for h in range(HEADS):
        ahead.append((h, scores(h)))
        if len(ahead) > 2:
            mix(*ahead.pop(0))
    for item in ahead:
        mix(*item)


def attend_scratch():
    count = WIN**3
    half = pltpu.VMEM((EMBED_SPAN, count), BF16)
    return [pltpu.VMEM((count, EMBED_SPAN), BF16), half, half, half, pltpu.VMEM((HEADS, count), F32), pltpu.VMEM((EMBED_SPAN, 128), F32)]


def whole_kernel(x_ref, car_ref, glob_ref, wk_ref, wqt_ref, wvt_ref, wo_ref, out_ref, inner_s, gl_s, *scratch):
    gl_s[...] = jnp.broadcast_to(glob_ref[0, 0:1, :], (128, EMBED_SPAN)).T

    def write(rows, local):
        inner_s[rows, :] = (local + widen(gl_s[rows, :], local.shape[1])).astype(BF16)

    attend(x_ref, car_ref, wk_ref, wqt_ref, wvt_ref, *scratch, write)
    update = lax.dot_general(inner_s[...], wo_ref[...], TN, preferred_element_type=F32)
    out_ref[...] = update.astype(BF16).reshape(out_ref.shape)


def whole_attention(grouped, own, glob, weights, wqt, wvt, w_out):
    rows, tokens, width = grouped.shape
    cell = WIN * WIN
    count = rows * cell
    cube = pl.BlockSpec((rows, cell, width), lambda i: (0, i, 0))
    row = pl.BlockSpec((1, 8, width), lambda i: (i, 0, 0))
    whole = pl.BlockSpec((width, width), lambda i: (0, 0))
    return pl.pallas_call(
        whole_kernel,
        grid=(tokens // cell,),
        in_specs=[cube, row, row, pl.BlockSpec((width, width), lambda i: (0, 1)), whole, whole, whole],
        out_specs=cube,
        out_shape=jax.ShapeDtypeStruct(grouped.shape, BF16),
        scratch_shapes=[pltpu.VMEM((width, count), BF16), pltpu.VMEM((width, 128), F32)] + attend_scratch(),
        compiler_params=PARAMS,
        cost_estimate=cost(17_000_000_000, 6 << 20, 8 << 20),
    )(grouped, own, glob, weights, wqt, wvt, w_out)


def carrier_match(all_ref, w_ref):
    match = jnp.dot(all_ref[...], w_ref[:, EMBED_SPAN:], preferred_element_type=F32).astype(BF16)
    return match[:, :EMBED_SPAN], match[:, EMBED_SPAN:]


def carrier_attention(own, w_ref, keys, values):
    mask = head_mask(HEADS)
    own = jnp.broadcast_to(own, (16, EMBED_SPAN)).astype(BF16)
    queries = jnp.dot(own, w_ref[:, :EMBED_SPAN], preferred_element_type=F32)
    queries = jnp.where(mask, queries, 0.0).astype(BF16)
    s = lax.dot_general(queries, keys, NT, preferred_element_type=F32) * SCALE
    weights = jnp.exp(s - jnp.max(s, axis=-1, keepdims=True))
    total = jnp.sum(weights, axis=-1, keepdims=True)
    summed = jnp.dot(weights.astype(BF16), values, preferred_element_type=F32) / total
    return jnp.sum(jnp.where(mask, summed, 0.0), axis=0, keepdims=True)


def glob_kernel(all_ref, own_ref, w_ref, out_ref):
    keys, values = carrier_match(all_ref, w_ref)
    for c in range(out_ref.shape[0]):
        out_ref[c] = jnp.broadcast_to(carrier_attention(own_ref[c, 0:1, :], w_ref, keys, values), out_ref.shape[1:])


def glob_of(carriers, own, weights):
    return pl.pallas_call(
        glob_kernel,
        out_shape=jax.ShapeDtypeStruct(own.shape, F32),
        compiler_params=PARAMS,
        cost_estimate=cost(400_000_000, 2 << 20, 16384),
    )(carriers, own, weights)


def spread_kernel(all_ref, mine_ref, w_ref, wo_ref, out_ref):
    keys, values = carrier_match(all_ref, w_ref)
    cubes = mine_ref.shape[0]
    queries = jnp.dot(mine_ref[...], w_ref[:, :EMBED_SPAN], preferred_element_type=F32)
    queries = jnp.broadcast_to(queries[:, None, :], (cubes, HEADS, EMBED_SPAN)).reshape(cubes * HEADS, EMBED_SPAN)
    mask = head_mask(cubes * HEADS)
    queries = jnp.where(mask, queries, 0.0).astype(BF16)
    s = lax.dot_general(queries, keys, NT, preferred_element_type=F32) * SCALE
    weights = jnp.exp(s - jnp.max(s, axis=-1, keepdims=True))
    total = jnp.sum(weights, axis=-1, keepdims=True)
    summed = jnp.dot(weights.astype(BF16), values, preferred_element_type=F32) / total
    glob = jnp.sum(jnp.where(mask, summed, 0.0).reshape(cubes, HEADS, EMBED_SPAN), axis=1)
    high = glob.astype(BF16)
    low = (glob - high.astype(F32)).astype(BF16)
    out_ref[...] = jnp.dot(high, wo_ref[...], preferred_element_type=F32) + jnp.dot(low, wo_ref[...], preferred_element_type=F32)


def row_glob(carriers, mine, weights, w_out):
    return pl.pallas_call(
        spread_kernel,
        out_shape=jax.ShapeDtypeStruct(mine.shape, F32),
        compiler_params=PARAMS,
        cost_estimate=cost(800_000_000, 3 << 20, 65536),
    )(carriers, mine, weights, w_out)


def add_kernel(x_ref, g_ref, out_ref):
    rows, tokens, width = x_ref.shape
    cells = g_ref.shape[1]
    x = x_ref[...].astype(F32).reshape(rows, cells, tokens // cells, width)
    out_ref[...] = (x + g_ref[...][:, :, None, :]).astype(BF16).reshape(x_ref.shape)


def add_glob(returned, glob):
    dests, tokens, width = returned.shape
    steps = 2
    block = pl.BlockSpec((dests // steps, tokens, width), lambda i: (i, 0, 0))
    return pl.pallas_call(
        add_kernel,
        grid=(steps,),
        in_specs=[block, pl.BlockSpec((dests // steps,) + glob.shape[1:], lambda i: (i, 0, 0))],
        out_specs=block,
        out_shape=jax.ShapeDtypeStruct(returned.shape, BF16),
        compiler_params=PARAMS,
        cost_estimate=cost(1_000_000, 2 << 20),
    )(returned, glob)


def exchange(values, axis, groups=None):
    return lax.all_to_all(values, axis, split_axis=0, concat_axis=0, tiled=True, axis_index_groups=groups)


def spread(values, axis):
    return exchange(jnp.broadcast_to(values[None], (lax.axis_size(axis),) + values.shape), axis)


def slab_first(rows, weights, w_out, groups, window):
    dests, tokens, width = rows.shape
    cells = tokens // (WIN * WIN)
    (normed,) = normalize(rows, False)
    grouped = exchange(normed, "window", groups)
    own, copies = own_carriers(grouped, cells, window)
    wqt, wvt = turn(weights)
    near = exchange(copies, "window").reshape(-1, width)
    update = whole_attention(grouped, own, jnp.zeros_like(own), weights, wqt, wvt, w_out)
    update, near = lax.optimization_barrier((update, near))
    returned = exchange(update, "window", groups)
    carriers = gather_inline(near)
    cubes = dests * cells
    mine = lax.dynamic_slice_in_dim(near, lax.axis_index("window") // WIN * cubes, cubes, 0)
    return returned, row_glob(carriers, mine, weights, w_out).reshape(dests, cells, width)


def carriers_first(rows, weights, w_out, groups, window):
    normed, sums = normalize(rows, True)
    width = normed.shape[-1]
    own, copies = own_carriers(exchange(sums, "window", groups), sums.shape[1], window)
    near = exchange(copies, "window").reshape(-1, width)
    normed, near = lax.optimization_barrier((normed, near))
    grouped = exchange(normed, "window", groups)
    wqt, wvt = turn(weights)
    carriers = gather_inline(near)
    glob = glob_of(carriers, own, weights)
    update = whole_attention(grouped, own, glob, weights, wqt, wvt, w_out)
    return exchange(update, "window", groups), jnp.zeros_like(sums)


def gather_inline(rows):
    count = lax.axis_size("inline")
    step = 1
    while step < count:
        other = lax.ppermute(rows, "inline", [(i, i ^ step) for i in range(count)])
        rows = jnp.concatenate([rows, other], axis=0)
        step *= 2
    return rows


def body(tokens, weights, w_out):
    window = lax.axis_size("window")
    width = tokens.shape[-1]
    groups = [[h * WIN + l for l in range(WIN)] for h in range(window // WIN)]
    rows = tokens.reshape(WIN, -1, width)
    returned, glob = lax.cond(
        lax.axis_index("replica") % 2 == 0,
        lambda *args: slab_first(*args, groups, window),
        lambda *args: carriers_first(*args, groups, window),
        rows, weights, w_out,
    )
    return add_glob(returned, glob).reshape(tokens.shape)


def solution(mesh):
    return jax.shard_map(
        body,
        mesh=mesh,
        in_specs=(P(("replica", "inline", "window"), None, None, None), P(), P()),
        out_specs=P(("replica", "inline", "window"), None, None, None),
        check_vma=False,
    )
```
